128 devices in a mesh: node: 16 (over y, x), local: 8 (over z, core).
Axes of the slice: x: 4, y: 4, z: 4, core: 2. Of those that a mesh axis runs over, the one named last changes fastest.
Arguments:
- tokens: bfloat16 [2048, 7168], P('node', 'local'), may hold values from -6 to 6
- out_grad: bfloat16 [2048, 7168], P('node', 'local'), may hold values from -6 to 6
- expert_ids: int32 [2048, 8], P('node'), may hold values from 0 to 31, as said below
- gates: float32 [2048, 8], P('node'), may hold values from 0.05 to 1
- gate_weight: bfloat16 [32, 7168, 1024], P('node', 'local'), may hold values from -0.0625 to 0.0625
- up_weight: bfloat16 [32, 7168, 1024], P('node', 'local'), may hold values from -0.0625 to 0.0625
- down_weight: bfloat16 [32, 1024, 7168], P('node', None, 'local'), may hold values from -0.1875 to 0.1875
Outputs:
- grad_tokens: bfloat16 [2048, 7168], P('node', 'local')
- gate_grad: bfloat16 [32, 7168, 1024], P('node', 'local')
- up_grad: bfloat16 [32, 7168, 1024], P('node', 'local')
- down_grad: bfloat16 [32, 1024, 7168], P('node', None, 'local')
The draws below stay inside these ranges and needn't reach their ends.
Inputs may be any that keep to these rules, and one draw needn't show every extreme that they name: `expert_ids`: each row names 8 different experts, all within at most 4 routing groups, group g being experts g * 4 to g * 4 + 3.
All inputs are finite; a program needn't handle non-finite values.
Results may differ from the reference program's by a relative error of at most 0.029.
Values may be sent and summed in bfloat16 or wider, within the bound.
No kernel may reach another device: no remote copies, remote signals or barrier semaphores. Data moves between devices by JAX's collectives and lax.ppermute only.
A program may use at most 128 MiB of HBM per device.

```python
import math
import jax
import jax.numpy as jnp
from jax import lax

D = 7168
F = 1024
TOP = 8
GROUP_EXP = 4
LIMIT = 4
TOK_NODE = 128
EXPERTS = 32
TOKENS = 2048
CAP = 40
N_NODE = 16
N_LOCAL = 8


def draw_expert_ids(key, part):
    key = jax.random.fold_in(key, 11)
    key_a, key_b, key_c, key_d = jax.random.split(key, 4)
    group_count = EXPERTS // GROUP_EXP
    group_bias = jax.random.randint(key_a, (group_count,), 0, 4) * 262144
    group_score = (jax.random.randint(key_b, (TOKENS, group_count), 0, 1048576) + group_bias[None, :]) * group_count
    group_score = group_score + jnp.arange(group_count, dtype=jnp.int32)[None, :]
    _, chosen = lax.top_k(group_score, LIMIT)
    allowed = jnp.any(chosen[:, :, None] == jnp.arange(group_count, dtype=jnp.int32)[None, None, :], axis=1)
    allowed_experts = jnp.repeat(allowed, GROUP_EXP, axis=1)
    expert_bias = jax.random.randint(key_c, (EXPERTS,), 0, 4) * 262144
    expert_score = (jax.random.randint(key_d, (TOKENS, EXPERTS), 0, 1048576) + expert_bias[None, :]) * EXPERTS
    expert_score = expert_score + jnp.arange(EXPERTS, dtype=jnp.int32)[None, :]
    expert_score = jnp.where(allowed_experts, expert_score, -1)
    _, picked = lax.top_k(expert_score, TOP)
    return picked.astype(jnp.int32)


def block_scale(rng, shape, pieces, low, high):
    gain = 1.0
    for axis_at, parts in pieces:
        steps = jax.random.uniform(jax.random.fold_in(jax.random.fold_in(rng, 6), axis_at), (parts,), jnp.float32, low / len(pieces), high / len(pieces))
        gain = gain * jnp.repeat(jnp.exp(steps), shape[axis_at] // parts).reshape((-1,) + (1,) * (len(shape) - 1 - axis_at))
    return gain


def gaussian(rng, dims, deviation, reach, pieces=(), held_as=jnp.bfloat16):
    level = block_scale(rng, dims, pieces, -0.22, 0.18) if pieces else 1.0
    result = jax.random.normal(rng, dims, jnp.float32) * deviation * level
    return jnp.minimum(jnp.maximum(result, -reach), reach).astype(held_as)


def setup_inputs(seed: int = 0) -> dict:
    key_of = jax.random.split(jax.random.key(seed), 8)
    return {
        "tokens": gaussian(key_of[0], (TOKENS, D), 1.0, 6.0, ((0, 16), (1, 8))),
        "out_grad": gaussian(key_of[1], (TOKENS, D), 1.0, 6.0, ((0, 16), (1, 8))),
        "expert_ids": draw_expert_ids(jax.random.fold_in(key_of[7], 71), 0),
        "gates": jnp.clip(jnp.exp(math.log(1.0) - 2.9957323 * jax.random.uniform(key_of[3], (TOKENS, TOP), jnp.float32) ** block_scale(key_of[3], (TOKENS, TOP), ((0, 16),), -0.2, 0.2)), 0.05, 1.0),
        "gate_weight": gaussian(key_of[4], (EXPERTS, D, F), D ** -0.5, 0.0625, ((0, 16), (1, 8))),
        "up_weight": gaussian(key_of[5], (EXPERTS, D, F), D ** -0.5, 0.0625, ((0, 16), (1, 8))),
        "down_weight": gaussian(key_of[6], (EXPERTS, F, D), F ** -0.5, 0.1875, ((0, 16), (2, 8))),
    }


def swiglu_backward(gate_pre, up_pre, grad_hidden):
    sigmoid_g = jax.nn.sigmoid(gate_pre)
    activated = gate_pre * sigmoid_g
    hidden_act = (activated * up_pre).astype(jnp.bfloat16)
    grad_gate = (grad_hidden * up_pre * sigmoid_g * (1.0 + gate_pre * (1.0 - sigmoid_g))).astype(jnp.bfloat16)
    grad_up = (grad_hidden * activated).astype(jnp.bfloat16)
    return hidden_act, grad_gate, grad_up


def rounded_term(value):
    return lax.optimization_barrier(value.astype(jnp.bfloat16)).astype(jnp.float32)


def expert_step(operands):
    x_rows, dy_rows, w_gate, w_up, w_down = operands
    width_slice = D // N_LOCAL
    gate_pre = jnp.zeros((x_rows.shape[0], F), jnp.float32)
    up_pre = jnp.zeros((x_rows.shape[0], F), jnp.float32)
    grad_hidden = jnp.zeros((x_rows.shape[0], F), jnp.float32)
    for piece in range(N_LOCAL):
        lower = piece * width_slice
        upper = lower + width_slice
        gate_pre = gate_pre + rounded_term(jnp.dot(x_rows[:, lower:upper], w_gate[lower:upper], preferred_element_type=jnp.float32))
        up_pre = up_pre + rounded_term(jnp.dot(x_rows[:, lower:upper], w_up[lower:upper], preferred_element_type=jnp.float32))
        grad_hidden = grad_hidden + rounded_term(jnp.dot(dy_rows[:, lower:upper], w_down[:, lower:upper].T, preferred_element_type=jnp.float32))
    hidden_act, grad_gate, grad_up = swiglu_backward(gate_pre, up_pre, grad_hidden)
    down_part = jnp.dot(hidden_act.T, dy_rows, preferred_element_type=jnp.float32).astype(jnp.bfloat16)
    gate_part = jnp.dot(x_rows.T, grad_gate, preferred_element_type=jnp.float32).astype(jnp.bfloat16)
    up_part = jnp.dot(x_rows.T, grad_up, preferred_element_type=jnp.float32).astype(jnp.bfloat16)
    grad_rows = (jnp.dot(grad_gate, w_gate.T, preferred_element_type=jnp.float32)
                 + jnp.dot(grad_up, w_up.T, preferred_element_type=jnp.float32)).astype(jnp.bfloat16)
    return grad_rows, gate_part, up_part, down_part


def reference(tokens, out_grad, expert_ids, gates, gate_weight, up_weight, down_weight):
    block_ids = expert_ids.reshape(N_NODE, TOK_NODE * TOP)
    onehot = (block_ids[:, :, None] == jnp.arange(EXPERTS, dtype=jnp.int32)[None, None, :]).astype(jnp.int32)
    earlier = jnp.cumsum(onehot, axis=1) - onehot
    slot_pos = jnp.sum(earlier * onehot, axis=2)
    kept_mask = slot_pos < CAP
    row_count = N_NODE * CAP
    block_index = jnp.arange(N_NODE, dtype=jnp.int32)[:, None]
    dest_row = jnp.where(kept_mask, block_ids * row_count + block_index * CAP + slot_pos, EXPERTS * row_count)
    dest_row = dest_row.reshape(-1).astype(jnp.int32)
    x_rep = jnp.repeat(tokens, TOP, axis=0)
    dy_rep = (gates.reshape(-1, 1) * jnp.repeat(out_grad, TOP, axis=0).astype(jnp.float32)).astype(jnp.bfloat16)
    blank = jnp.zeros((EXPERTS * row_count, D), jnp.bfloat16)
    x_buf = blank.at[dest_row].set(x_rep, mode="drop").reshape(EXPERTS, row_count, D)
    dy_buf = blank.at[dest_row].set(dy_rep, mode="drop").reshape(EXPERTS, row_count, D)
    grad_rows, gate_grad, up_grad, down_grad = lax.map(expert_step, (x_buf, dy_buf, gate_weight, up_weight, down_weight))
    back_rows = grad_rows.reshape(EXPERTS * row_count, D)
    safe_row = jnp.minimum(dest_row, EXPERTS * row_count - 1)
    picked = jnp.where(kept_mask.reshape(-1, 1), back_rows[safe_row].astype(jnp.float32), jnp.float32(0.0))
    grad_tokens = picked.reshape(TOKENS, TOP, D).sum(axis=1).astype(jnp.bfloat16)
    return grad_tokens, gate_grad, up_grad, down_grad
```

```python
import functools
import jax
import jax.numpy as jnp
from jax import lax
from jax.experimental import pallas as pl
from jax.experimental.pallas import tpu as pltpu
from jax.sharding import PartitionSpec as P

BF = jnp.bfloat16
F32 = jnp.float32
MIB = 1024 * 1024
NN = (((1,), (0,)), ((), ()))
NT = (((1,), (1,)), ((), ()))
TN = (((0,), (0,)), ((), ()))


def dot(a, b, dims):
    return lax.dot_general(a, b, dims, preferred_element_type=F32)


def params(mib):
    return pltpu.CompilerParams(vmem_limit_bytes=mib * MIB)


def cost(flops, moved):
    return pl.CostEstimate(flops=flops, bytes_accessed=moved, transcendentals=0)


def whole(shape):
    return pl.BlockSpec(shape, lambda *_: (0,) * len(shape))


def slot_map(ids, gates):
    tok, top = ids.shape
    lane = lax.broadcasted_iota(jnp.int32, (tok, tok), 1)
    row = lax.broadcasted_iota(jnp.int32, (tok, tok), 0)
    named = jnp.zeros((tok, tok), F32)
    weight = jnp.zeros((tok, tok), F32)
    for k in range(top):
        hit = ids[:, k : k + 1] == lane
        named = jnp.where(hit, 1.0, named)
        weight = jnp.where(hit, gates[:, k : k + 1], weight)
    named_t = named.T
    before = (row < lane).astype(BF)
    pos = dot(named_t.astype(BF), before, NN)
    return jnp.where(named_t > 0.0, pos, -1.0), weight.T


def one_hot(pos, e, cap, exp_local, nodes):
    slot = lax.broadcasted_iota(jnp.int32, (cap, pos.shape[1]), 0).astype(F32)
    return jnp.concatenate(
        [
            (pos[n * exp_local + e : n * exp_local + e + 1, :] == slot).astype(F32)
            for n in range(nodes)
        ],
        axis=0,
    )


def pack_kernel(e, cap, exp_local, nodes, ids_ref, gates_ref, tok_ref, grad_ref, out_ref, pos_ref):
    pos, weight = slot_map(ids_ref[...], gates_ref[...])
    pos_ref[...] = pos
    width = tok_ref.shape[1]
    sel = one_hot(pos, e, cap, exp_local, nodes)
    scale = jnp.concatenate(
        [
            jnp.sum(
                sel[n * cap : (n + 1) * cap]
                * weight[n * exp_local + e : n * exp_local + e + 1, :],
                axis=1,
                keepdims=True,
            )
            for n in range(nodes)
        ],
        axis=0,
    )
    sel = sel.astype(BF)
    out_ref[:, :width] = dot(sel, tok_ref[...], NN).astype(BF)
    out_ref[:, width:] = (scale * dot(sel, grad_ref[...], NN)).astype(BF)


def pack(e, cap, exp_local, nodes, ids, gates, tokens, out_grad):
    tok, width = tokens.shape
    rows = nodes * cap
    return pl.pallas_call(
        functools.partial(pack_kernel, e, cap, exp_local, nodes),
        out_shape=(
            jax.ShapeDtypeStruct((rows, 2 * width), BF),
            jax.ShapeDtypeStruct((tok, tok), F32),
        ),
        compiler_params=params(24),
        cost_estimate=cost(4 * rows * tok * width, 4 * rows * width + 4 * tok * width),
        name="pack",
    )(ids, gates, tokens, out_grad)


def ring_slot(half, j):
    if half == 0:
        return jnp.where(j == 0, 6, jnp.where(j == 1, 4, jnp.where(j == 2, 0, 3)))
    return jnp.where(j == 0, 7, jnp.where(j == 1, 1, jnp.where(j == 2, 2, 5)))


def products_kernel(blk, place, rows_ref, wg_ref, wu_ref, wd_ref, own_ref, other_ref):
    half = pl.program_id(0)
    z, core = place[0], place[1]
    rows, width2 = rows_ref.shape
    width = width2 // 2
    x = rows_ref[:, :width]
    dy = rows_ref[:, width:]
    vals = (
        dot(x, wg_ref[0], NN).astype(BF),
        dot(x, wu_ref[0], NN).astype(BF),
        dot(dy, wd_ref[0], NT).astype(BF),
    )
    for q in range(rows // blk):
        j = lax.rem(q // 2 - z + 4, 4)
        slot = jnp.where(half == 0, ring_slot(0, j), ring_slot(1, j))

        def put(ref, q=q, slot=slot):
            for k in range(3):
                ref[slot, k] = vals[k][q * blk : (q + 1) * blk]

        pl.when(core == q % 2)(functools.partial(put, own_ref))
        pl.when(core != q % 2)(functools.partial(put, other_ref))


def products(e, blk, place, rows_x_dy, wg, wu, wd):
    rows, width2 = rows_x_dy.shape
    width = width2 // 2
    hidden = wg.shape[2]
    hh = hidden // 2
    out = jax.ShapeDtypeStruct((8, 3, blk, hh), BF)
    return pl.pallas_call(
        functools.partial(products_kernel, blk),
        out_shape=(out, out),
        grid_spec=pltpu.PrefetchScalarGridSpec(
            num_scalar_prefetch=1,
            grid=(2,),
            in_specs=[
                whole((rows, width2)),
                pl.BlockSpec((1, width, hh), lambda h, _: (e, 0, h)),
                pl.BlockSpec((1, width, hh), lambda h, _: (e, 0, h)),
                pl.BlockSpec((1, hh, width), lambda h, _: (e, h, 0)),
            ],
            out_specs=[whole(out.shape), whole(out.shape)],
        ),
        compiler_params=params(40),
        cost_estimate=cost(6 * rows * width * hidden, 6 * width * hidden + 10 * rows * width),
        name="products",
    )(place, rows_x_dy, wg, wu, wd)


def swiglu_kernel(kept_ref, rm_ref, rp_ref, sp_ref, sm_ref, out_ref):
    for half, (direct, ringed) in enumerate(((rm_ref, sp_ref), (rp_ref, sm_ref))):
        tot = [
            kept_ref[2 + half, k].astype(F32)
            + direct[1, k].astype(F32)
            + ringed[k].astype(F32)
            for k in range(3)
        ]
        gate, up, gh = tot
        sig = jax.nn.sigmoid(gate)
        act = gate * sig
        out_ref[half, 0] = (act * up).astype(BF)
        out_ref[half, 1] = (gh * up * sig * (1.0 + gate * (1.0 - sig))).astype(BF)
        out_ref[half, 2] = (gh * act).astype(BF)


def swiglu(kept, rm, rp, sp, sm):
    shape = (2,) + kept.shape[1:]
    return pl.pallas_call(
        swiglu_kernel,
        out_shape=jax.ShapeDtypeStruct(shape, BF),
        compiler_params=params(24),
        cost_estimate=cost(0, 8 * kept.size),
        name="swiglu",
    )(kept, rm, rp, sp, sm)


def move(x, dz, dcore=0):
    return lax.ppermute(
        x, "local", [(i, ((i // 2 + dz) % 4) * 2 + (i + dcore) % 2) for i in range(8)]
    )


def sum_over_width(own, other):
    got = move(other, 0, 1)
    to_next = own[0:2] + got[0:2]
    to_prev = own[2:4] + got[2:4]
    kept = own[4:8] + got[4:8]
    rp = move(to_next, 1)
    rm = move(to_prev, -1)
    sp = move(kept[0] + rp[0], 1)
    sm = move(kept[1] + rm[0], -1)
    return swiglu(kept, rm, rp, sp, sm)


def gather_rows(mine):
    prev = move(mine, 1)
    nxt = move(mine, -1)
    far0 = move(prev[0], 1)
    far1 = move(nxt[1], -1)
    parts = (mine, prev, nxt, far0, far1)
    return parts + tuple(move(p, 0, 1) for p in parts)


def grad_rows_kernel(blk, place, *refs):
    parts, (wg_ref, wu_ref), (out_ref, h_ref, acc_ref) = refs[:10], refs[10:12], refs[12:]
    f = pl.program_id(0)
    hh = h_ref.shape[2] // 2
    z, core = place[0], place[1]

    @pl.when(f == 0)
    def _():
        for c in range(2):
            mine, prev, nxt, far0, far1 = parts[5 * c : 5 * c + 5]
            for j in range(4):
                q = lax.rem(z + j, 4) * 2 + lax.rem(core + c, 2)
                at = pl.ds(pl.multiple_of(q * blk, 16), blk)
                for half in range(2):
                    for k in range(3):
                        if j == 2:
                            val = (far0, far1)[half][k]
                        else:
                            val = (mine, nxt, None, prev)[j][half, k]
                        h_ref[k, at, half * hh : (half + 1) * hh] = val

    def part(half):
        cols = slice(half * hh, (half + 1) * hh)
        return dot(h_ref[1, :, cols], wg_ref[0], NT) + dot(h_ref[2, :, cols], wu_ref[0], NT)

    @pl.when(f == 0)
    def _():
        acc_ref[...] = part(0)

    @pl.when(f == 1)
    def _():
        out_ref[...] = (acc_ref[...] + part(1)).astype(BF)


def grad_rows(e, blk, rows, place, parts, wg, wu):
    width, hidden = wg.shape[1:]
    hh = hidden // 2
    return pl.pallas_call(
        functools.partial(grad_rows_kernel, blk),
        out_shape=(
            jax.ShapeDtypeStruct((rows, width), BF),
            jax.ShapeDtypeStruct((3, rows, hidden), BF),
        ),
        grid_spec=pltpu.PrefetchScalarGridSpec(
            num_scalar_prefetch=1,
            grid=(2,),
            in_specs=[whole(p.shape) for p in parts]
            + [pl.BlockSpec((1, width, hh), lambda f, _: (e, 0, f))] * 2,
            out_specs=[whole((rows, width)), whole((3, rows, hidden))],
            scratch_shapes=[pltpu.VMEM((rows, width), F32)],
        ),
        compiler_params=params(40),
        cost_estimate=cost(4 * rows * width * hidden, 4 * width * hidden + 14 * rows * hidden),
        name="grad_rows",
    )(place, *parts, wg, wu)


def weight_grads_kernel(h_ref, rows_ref, *refs):
    dg_ref, du_ref, dd_ref = refs[-3:]
    width = rows_ref.shape[1] // 2
    x = rows_ref[:, :width]
    dg_ref[0] = dot(x, h_ref[1], TN).astype(BF)
    du_ref[0] = dot(x, h_ref[2], TN).astype(BF)
    dd_ref[0] = dot(h_ref[0], rows_ref[:, width:], TN).astype(BF)


def weight_grads(e, exp_local, h, rows_x_dy, into):
    rows, width2 = rows_x_dy.shape
    width, hidden = width2 // 2, h.shape[2]
    hh = hidden // 2
    up = jax.ShapeDtypeStruct((exp_local, width, hidden), BF)
    down = jax.ShapeDtypeStruct((exp_local, hidden, width), BF)
    return pl.pallas_call(
        weight_grads_kernel,
        out_shape=(up, up, down),
        grid=(2,),
        in_specs=[
            pl.BlockSpec((3, rows, hh), lambda f: (0, 0, f)),
            whole((rows, width2)),
        ]
        + [pl.BlockSpec(memory_space=pl.ANY)] * len(into),
        out_specs=[
            pl.BlockSpec((1, width, hh), lambda f: (e, 0, f)),
            pl.BlockSpec((1, width, hh), lambda f: (e, 0, f)),
            pl.BlockSpec((1, hh, width), lambda f: (e, f, 0)),
        ],
        input_output_aliases={2 + i: i for i in range(len(into))},
        compiler_params=params(40),
        cost_estimate=cost(6 * rows * width * hidden, 6 * width * hidden + 10 * rows * hidden),
        name="weight_grads",
    )(h, rows_x_dy, *into)


def combine_kernel(cap, exp_local, nodes, pos_ref, *refs):
    backs, out_ref = refs[:-1], refs[-1]
    pos = pos_ref[...]
    sel = [one_hot(pos, e, cap, exp_local, nodes).astype(BF) for e in range(exp_local)]
    tot = dot(sel[0], backs[0][...], TN)
    for e in range(1, exp_local):
        tot = tot + dot(sel[e], backs[e][...], TN)
    out_ref[...] = tot.astype(BF)


def combine(cap, exp_local, nodes, pos, backs):
    tok = pos.shape[0]
    rows, width = backs[0].shape
    return pl.pallas_call(
        functools.partial(combine_kernel, cap, exp_local, nodes),
        out_shape=jax.ShapeDtypeStruct((tok, width), BF),
        compiler_params=params(24),
        cost_estimate=cost(4 * rows * tok * width, 4 * rows * width),
        name="combine",
    )(pos, *backs)


def on_device(tokens, out_grad, expert_ids, gates, gate_weight, up_weight, down_weight):
    tok, width = tokens.shape
    top = expert_ids.shape[1]
    nodes = lax.axis_size("node")
    exp_local = gate_weight.shape[0]
    cap = tok * top * 5 // (exp_local * nodes * 4)
    rows = nodes * cap
    blk = rows // 8
    local = lax.axis_index("local")
    place = jnp.stack([local // 2, local % 2]).astype(jnp.int32)

    got, pos = [], None
    for e in range(exp_local):
        sent, pos_e = pack(e, cap, exp_local, nodes, expert_ids, gates, tokens, out_grad)
        pos = pos_e if pos is None else pos
        got.append(lax.all_to_all(sent, "node", split_axis=0, concat_axis=0, tiled=True))

    grads, backs = (), []
    for e in range(exp_local):
        own, other = products(e, blk, place, got[e], gate_weight, up_weight, down_weight)
        mine = sum_over_width(own, other)
        parts = gather_rows(mine)
        out_rows, h = grad_rows(e, blk, rows, place, parts, gate_weight, up_weight)
        backs.append(lax.all_to_all(out_rows, "node", split_axis=0, concat_axis=0, tiled=True))
        grads = weight_grads(e, exp_local, h, got[e], grads)
    grad_tokens = combine(cap, exp_local, nodes, pos, backs)
    return (grad_tokens,) + tuple(grads)


def solution(mesh):
    return jax.shard_map(
        on_device,
        mesh=mesh,
        in_specs=(
            P("node", "local"),
            P("node", "local"),
            P("node", None),
            P("node", None),
            P("node", "local", None),
            P("node", "local", None),
            P("node", None, "local"),
        ),
        out_specs=(
            P("node", "local"),
            P("node", "local", None),
            P("node", "local", None),
            P("node", None, "local"),
        ),
        check_vma=False,
    )
```

```python
import functools
import jax
import jax.numpy as jnp
from jax import lax
from jax.experimental import pallas as pl
from jax.experimental.pallas import tpu as pltpu
from jax.sharding import PartitionSpec as P

BF = jnp.bfloat16
F32 = jnp.float32
MIB = 1024 * 1024
BIG = 20
NN = (((1,), (0,)), ((), ()))
NT = (((1,), (1,)), ((), ()))
TN = (((0,), (0,)), ((), ()))


def dot(a, b, dims):
    return lax.dot_general(a, b, dims, preferred_element_type=F32)


def params(mib):
    return pltpu.CompilerParams(vmem_limit_bytes=mib * MIB)


def cost(flops, moved):
    return pl.CostEstimate(flops=flops, bytes_accessed=moved, transcendentals=0)


def whole(shape):
    return pl.BlockSpec(shape, lambda *_: (0,) * len(shape))


ANY = pl.BlockSpec(memory_space=pl.ANY)
VM = pl.BlockSpec(memory_space=pltpu.VMEM)
SM = pl.BlockSpec(memory_space=pltpu.SMEM)


def copy(src, dst, sems, i):
    c = pltpu.make_async_copy(src, dst, sems.at[i])
    c.start()
    return c


def in_hbm(x):
    return pltpu.with_memory_space_constraint(x, pltpu.HBM)


def slot_map(ids, gates, experts):
    top, tok = ids.shape
    row = lax.broadcasted_iota(jnp.int32, (experts, tok), 0)
    named = jnp.zeros((experts, tok), F32)
    weight = jnp.zeros((experts, tok), F32)
    for k in range(top):
        hit = ids[k : k + 1, :] == row
        named = jnp.where(hit, 1.0, named)
        weight = jnp.where(hit, gates[k : k + 1, :], weight)
    at = lax.broadcasted_iota(jnp.int32, (tok, tok), 0)
    before = (at < lax.broadcasted_iota(jnp.int32, (tok, tok), 1)).astype(BF)
    pos = dot(named.astype(BF), before, NN)
    return jnp.where(named > 0.0, pos, -1.0), weight


def one_hot(pos, e, cap, exp_local, nodes):
    slot = lax.broadcasted_iota(jnp.int32, (cap, pos.shape[1]), 0).astype(F32)
    return jnp.concatenate(
        [
            (pos[n * exp_local + e : n * exp_local + e + 1, :] == slot).astype(F32)
            for n in range(nodes)
        ],
        axis=0,
    )


def pack_kernel(cols, cap, exp_local, nodes, ids_ref, gates_ref, tok_ref, grad_ref, *refs):
    out_ref, pos_ref, out_val, sems = refs[-4:]
    outs = []
    pos, weight = slot_map(ids_ref[...], gates_ref[...], exp_local * nodes)
    pos_ref[...] = pos
    width = tok_ref.shape[1]
    for e in range(exp_local):
        if all(col[0] != e for col in cols):
            continue
        sel = one_hot(pos, e, cap, exp_local, nodes)
        sel_bf = sel.astype(BF)
        for i, (col_e, kind) in enumerate(cols):
            at = slice(i * width, (i + 1) * width)
            if col_e == e and kind == 0:
                out_val[:, at] = dot(sel_bf, tok_ref[...], NN).astype(BF)
                outs.append(copy(out_val.at[:, at], out_ref.at[:, at], sems, i))
            elif col_e == e:
                scale = jnp.concatenate(
                    [
                        jnp.sum(
                            sel[n * cap : (n + 1) * cap]
                            * weight[n * exp_local + e : n * exp_local + e + 1, :],
                            axis=1,
                            keepdims=True,
                        )
                        for n in range(nodes)
                    ],
                    axis=0,
                )
                out_val[:, at] = (scale * dot(sel_bf, grad_ref[...], NN)).astype(BF)
                outs.append(copy(out_val.at[:, at], out_ref.at[:, at], sems, i))
    for c in outs:
        c.wait()


def pack(cols, cap, exp_local, nodes, ids, gates, tokens, out_grad, after):
    tok, width = tokens.shape
    rows = nodes * cap
    return pl.pallas_call(
        functools.partial(pack_kernel, cols, cap, exp_local, nodes),
        out_shape=(
            pltpu.HBM((rows, len(cols) * width), BF),
            jax.ShapeDtypeStruct((exp_local * nodes, tok), F32),
        ),
        in_specs=[VM] * 4 + [ANY] * len(after),
        out_specs=(pl.BlockSpec(memory_space=pltpu.HBM), VM),
        scratch_shapes=[
            pltpu.VMEM((rows, len(cols) * width), BF),
            pltpu.SemaphoreType.DMA((len(cols),)),
        ],
        compiler_params=params(24),
        cost_estimate=cost(1, 1),
        name="pack",
    )(ids.T, gates.T, in_hbm(tokens), in_hbm(out_grad), *after)


def ring_slot(half, j):
    if half == 0:
        return jnp.where(j == 0, 6, jnp.where(j == 1, 4, jnp.where(j == 2, 0, 3)))
    return jnp.where(j == 0, 7, jnp.where(j == 1, 1, jnp.where(j == 2, 2, 5)))


def products_kernel(e, blk, ks, x_at, dy_at, n_after, place, x_ref, dy_ref, *refs):
    w_refs = refs[:3]
    own_ref, *other_refs, x, w, wd, stage, sems, out_sems = refs[3 + n_after :]
    z, core = place[0], place[1]
    rows, width = x.shape[1:]
    hh = wd.shape[1]
    cols = [slice(0, hh), slice(hh, 2 * hh)]

    def rows_copy(kind):
        ref, at = ((x_ref, x_at), (dy_ref, dy_at))[kind]
        return copy(ref.at[:, at * width : (at + 1) * width], x.at[kind], sems, kind)

    def weight_copies(k):
        if k == 2:
            return [copy(w_refs[2].at[e, cols[h]], wd.at[h], sems, 6 + h) for h in range(2)]
        return [copy(w_refs[k].at[e, :, cols[h]], w.at[k, h], sems, 2 + 2 * k + h) for h in range(2)]

    x_in = {ks[0] // 2: rows_copy(ks[0] // 2)}
    w_in = {ks[0]: weight_copies(ks[0])}
    outs = []
    for k in ks:
        for h in range(2):
            if h == 0 and k in (ks[0], 2):
                x_in[k // 2].wait()
            w_in[k][h].wait()
            if k == ks[0] and h == 0:
                for later in ks[1:]:
                    if later == 2:
                        x_in[1] = rows_copy(1)
                    w_in[later] = weight_copies(later)
            val = dot(x[k // 2], wd[h] if k == 2 else w[k, h], NT if k == 2 else NN).astype(BF)
            for q in range(rows // blk):
                slot = ring_slot(h, lax.rem(q // 2 - z + 4, 4))
                stage[lax.rem(q + core, 2), slot, k] = val[q * blk : (q + 1) * blk]
        outs.append(copy(
            stage.at[1, :, k],
            other_refs[0].at[:, k] if len(other_refs) == 1 else other_refs[k].at[:, 0],
            out_sems,
            2 * k + 1,
        ))
        outs.append(copy(stage.at[0, :, k], own_ref.at[:, k], out_sems, 2 * k))
    for c in outs:
        c.wait()


def products(e, blk, ks, place, x_rows, dy_rows, weights, after, pieces):
    (x_arr, x_at), (dy_arr, dy_at) = x_rows, dy_rows
    rows = x_arr.shape[0]
    width, hidden = weights[0].shape[1:]
    hh = hidden // 2
    out = jax.ShapeDtypeStruct((8, 3, blk, hh), BF)
    return pl.pallas_call(
        functools.partial(products_kernel, e, blk, ks, x_at, dy_at, len(after)),
        out_shape=(out,)
        + tuple(jax.ShapeDtypeStruct((8, 3 // pieces, blk, hh), BF) for _ in range(pieces)),
        in_specs=[SM] + [ANY] * (5 + len(after)),
        out_specs=[ANY] * (1 + pieces),
        scratch_shapes=[
            pltpu.VMEM((2, rows, width), BF),
            pltpu.VMEM((2, 2, width, hh), BF),
            pltpu.VMEM((2, hh, width), BF),
            pltpu.VMEM((2, 8, 3, blk, hh), BF),
            pltpu.SemaphoreType.DMA((8,)),
            pltpu.SemaphoreType.DMA((6,)),
        ],
        compiler_params=params(BIG),
        cost_estimate=cost(1, 1),
        name="products",
    )(place, in_hbm(x_arr), in_hbm(dy_arr), *[in_hbm(w) for w in weights], *after)


def swiglu_kernel(kept_ref, rm_ref, rp_ref, sp_ref, sm_ref, *refs):
    out_ref = refs[-1]
    for half, (direct, ringed) in enumerate(((rm_ref, sp_ref), (rp_ref, sm_ref))):
        gate, up, gh = [
            kept_ref[2 + half, k].astype(F32)
            + direct[1, k].astype(F32)
            + ringed[k].astype(F32)
            for k in range(3)
        ]
        sig = jax.nn.sigmoid(gate)
        act = gate * sig
        out_ref[half, 0] = (act * up).astype(BF)
        out_ref[half, 1] = (gh * up * sig * (1.0 + gate * (1.0 - sig))).astype(BF)
        out_ref[half, 2] = (gh * act).astype(BF)


def swiglu(kept, rm, rp, sp, sm, after):
    return pl.pallas_call(
        swiglu_kernel,
        out_shape=jax.ShapeDtypeStruct(rm.shape, BF),
        in_specs=[VM] * 5 + [ANY] * len(after),
        out_specs=VM,
        compiler_params=params(24),
        cost_estimate=cost(1, 1),
        name="swiglu",
    )(kept, rm, rp, sp, sm, *after)


def move(x, dz, dcore=0):
    return lax.ppermute(
        x, "local", [(i, ((i // 2 + dz) % 4) * 2 + (i + dcore) % 2) for i in range(8)]
    )


def fold_kernel(kept_ref, rp_ref, rm_ref, *refs):
    next_ref, prev_ref = refs[-2:]
    next_ref[...] = (kept_ref[0].astype(F32) + rp_ref[0].astype(F32)).astype(BF)
    prev_ref[...] = (kept_ref[1].astype(F32) + rm_ref[0].astype(F32)).astype(BF)


def fold(kept, rp, rm, after):
    out = jax.ShapeDtypeStruct(rp.shape[1:], BF)
    return pl.pallas_call(
        fold_kernel,
        out_shape=(out, out),
        in_specs=[VM] * 3 + [ANY] * len(after),
        out_specs=(VM, VM),
        compiler_params=params(24),
        cost_estimate=cost(1, 1),
        name="fold",
    )(kept, rp, rm, *after)


def add_kernel(pieces, own_ref, *refs):
    got_refs = refs[:pieces]
    outs = refs[pieces:]
    for out_ref, at in zip(outs, (0, 2, 4)):
        n = out_ref.shape[0]
        if pieces == 1:
            got = got_refs[0][at : at + n].astype(F32)
            out_ref[...] = (own_ref[at : at + n].astype(F32) + got).astype(BF)
        else:
            for k in range(3):
                got = got_refs[k][at : at + n, 0].astype(F32)
                out_ref[:, k] = (own_ref[at : at + n, k].astype(F32) + got).astype(BF)


def add(own, got):
    tail = own.shape[1:]
    return pl.pallas_call(
        functools.partial(add_kernel, len(got)),
        out_shape=tuple(jax.ShapeDtypeStruct((n,) + tail, BF) for n in (2, 2, 4)),
        compiler_params=params(24),
        cost_estimate=cost(1, 1),
        name="add",
    )(own, *got)


def sum_over_width(own, other, swap_after, last_after, pieces):
    if pieces == 1:
        other = (tie(other, *swap_after),) if swap_after else (other,)
    got = [move(piece, 0, 1) for piece in other]
    to_next, to_prev, kept = add(own, got)
    rp = move(to_next, 1)
    rm = move(to_prev, -1)
    add_next, add_prev = fold(kept, rp, rm, ())
    sp = move(add_next, 1)
    sm = move(add_prev, -1)
    return swiglu(kept, rm, rp, sp, sm, last_after), (sp, sm)


def tie_kernel(*refs):
    del refs


def tie(x, *others):
    return pl.pallas_call(
        tie_kernel,
        out_shape=jax.ShapeDtypeStruct(x.shape, x.dtype),
        in_specs=[ANY] * (1 + len(others)),
        out_specs=ANY,
        input_output_aliases={0: 0},
        compiler_params=params(BIG),
        cost_estimate=cost(1, 1),
        name="tie",
    )(x, *others)


def gather_rows(mine):
    prev = move(mine, 1)
    nxt = move(mine, -1)
    far0 = move(prev[0], 1)
    far1 = move(nxt[1], -1)
    parts = (mine, prev, nxt, far0, far1)
    return parts + tuple(move(p, 0, 1) for p in parts)


def place_rows(blk, z, core, parts, k, dst):
    for c in range(2):
        for i, j in enumerate((0, 3, 1, 2, 2)):
            q = lax.rem(z + j, 4) * 2 + lax.rem(core + c, 2)
            at = pl.ds(pl.multiple_of(q * blk, 16), blk)
            part = parts[5 * c + i]
            for half in range(2):
                for n in range(dst.shape[0]):
                    cols = slice(half * part.shape[-1], (half + 1) * part.shape[-1])
                    if i < 3:
                        dst[n, at, cols] = part[half, k + n]
                    elif half == i - 3:
                        dst[n, at, cols] = part[k + n]


def grad_rows_kernel(e, blk, place, *refs):
    parts = refs[:10]
    wg_ref, wu_ref, out_ref, h_ref, h_val, w, out_val, sems, out_sems = refs[10:]
    w_in = [copy(w_ref.at[e], w.at[n], sems, n) for n, w_ref in enumerate((wg_ref, wu_ref))]
    place_rows(blk, place[0], place[1], parts, 0, h_val)
    w_in[0].wait()
    tot = dot(h_val[1], w[0], NT)
    w_in[1].wait()
    outs = [copy(h_val, h_ref, out_sems, 0)]
    part = out_val.shape[0] // 2
    for m in range(2):
        at = slice(m * part, (m + 1) * part)
        out_val[at] = (tot[at] + dot(h_val[2, at], w[1], NT)).astype(BF)
        outs.append(copy(out_val.at[at], out_ref.at[at], out_sems, 1 + m))
    for c in outs:
        c.wait()


def grad_rows(e, blk, rows, place, parts, weights):
    width, hidden = weights[0].shape[1:]
    return pl.pallas_call(
        functools.partial(grad_rows_kernel, e, blk),
        out_shape=(
            pltpu.HBM((rows, width), BF),
            pltpu.HBM((3, rows, hidden), BF),
        ),
        in_specs=[SM] + [VM] * 10 + [ANY] * 2,
        out_specs=(pl.BlockSpec(memory_space=pltpu.HBM),) * 2,
        scratch_shapes=[
            pltpu.VMEM((3, rows, hidden), BF),
            pltpu.VMEM((2, width, hidden), BF),
            pltpu.VMEM((rows, width), BF),
            pltpu.SemaphoreType.DMA((2,)),
            pltpu.SemaphoreType.DMA((3,)),
        ],
        compiler_params=params(BIG),
        cost_estimate=cost(1, 1),
        name="grad_rows",
    )(place, *parts, *[in_hbm(w) for w in weights[:2]])


def weight_grads_kernel(e, x_at, dy_at, x_ref, dy_ref, h_ref, *refs):
    out_refs = refs[-9:-6]
    x, h_val, dgu, dd, sems, out_sems = refs[-6:]
    width = x.shape[2]
    hh = h_val.shape[2] // 2
    cols = [slice(0, hh), slice(hh, 2 * hh)]
    x_in = [copy(x_ref.at[:, x_at * width : (x_at + 1) * width], x.at[0], sems, 0)]
    h_in = {k: copy(h_ref.at[k], h_val.at[k], sems, 2 + k) for k in (1, 2, 0)}
    x_in.append(copy(dy_ref.at[:, dy_at * width : (dy_at + 1) * width], x.at[1], sems, 1))
    outs = []
    for k in (1, 2, 0):
        h_in[k].wait()
        if k != 2:
            x_in[0 if k == 1 else 1].wait()
        for h in range(2):
            if k == 0:
                dd[h] = dot(h_val[k, :, cols[h]], x[1], TN).astype(BF)
                outs.append(copy(dd.at[h], out_refs[2].at[e, cols[h]], out_sems, 4 + h))
            else:
                dgu[k - 1, h] = dot(x[0], h_val[k, :, cols[h]], TN).astype(BF)
                outs.append(
                    copy(dgu.at[k - 1, h], out_refs[k - 1].at[e, :, cols[h]], out_sems, 2 * k - 2 + h)
                )
    for c in outs:
        c.wait()


def weight_grads(e, exp_local, width, x_rows, dy_rows, hidden_vals, into):
    (x_arr, x_at), (dy_arr, dy_at) = x_rows, dy_rows
    rows, hidden = hidden_vals.shape[1:]
    hh = hidden // 2
    up = jax.ShapeDtypeStruct((exp_local, width, hidden), BF)
    down = jax.ShapeDtypeStruct((exp_local, hidden, width), BF)
    return pl.pallas_call(
        functools.partial(weight_grads_kernel, e, x_at, dy_at),
        out_shape=(up, up, down),
        in_specs=[ANY] * (3 + len(into)),
        out_specs=[ANY] * 3,
        scratch_shapes=[
            pltpu.VMEM((2, rows, width), BF),
            pltpu.VMEM((3, rows, hidden), BF),
            pltpu.VMEM((2, 2, width, hh), BF),
            pltpu.VMEM((2, hh, width), BF),
            pltpu.SemaphoreType.DMA((5,)),
            pltpu.SemaphoreType.DMA((6,)),
        ],
        input_output_aliases={3 + i: i for i in range(len(into))},
        compiler_params=params(BIG),
        cost_estimate=cost(1, 1),
        name="weight_grads",
    )(in_hbm(x_arr), in_hbm(dy_arr), in_hbm(hidden_vals), *into)


def combine_kernel(cap, exp_local, nodes, pos_ref, *refs):
    backs, out_ref = refs[:-1], refs[-1]
    pos = pos_ref[...]
    sel = [one_hot(pos, e, cap, exp_local, nodes).astype(BF) for e in range(exp_local)]
    tot = dot(sel[0], backs[0][...], TN)
    for e in range(1, exp_local):
        tot = tot + dot(sel[e], backs[e][...], TN)
    out_ref[...] = tot.astype(BF)


def combine(cap, exp_local, nodes, pos, backs):
    tok = pos.shape[1]
    rows, width = backs[0].shape
    return pl.pallas_call(
        functools.partial(combine_kernel, cap, exp_local, nodes),
        out_shape=jax.ShapeDtypeStruct((tok, width), BF),
        compiler_params=params(24),
        cost_estimate=cost(1, 1),
        name="combine",
    )(pos, *backs)


def on_device(tokens, out_grad, expert_ids, gates, gate_weight, up_weight, down_weight):
    tok, width = tokens.shape
    top = expert_ids.shape[1]
    nodes = lax.axis_size("node")
    exp_local = gate_weight.shape[0]
    cap = tok * top * 5 // (exp_local * nodes * 4)
    rows = nodes * cap
    blk = rows // 8
    local = lax.axis_index("local")
    place = jnp.stack([local // 2, local % 2]).astype(jnp.int32)

    weights = (gate_weight, up_weight, down_weight)
    def exchange(x):
        return lax.all_to_all(x, "node", split_axis=0, concat_axis=0, tiled=True)

    pack_args = (cap, exp_local, nodes, expert_ids, gates, tokens, out_grad)
    first, pos = pack(((0, 0), (0, 1)), *pack_args, (place,))
    second, packed = pack(((1, 0), (1, 1)), *pack_args, ())
    got = (exchange(first), exchange(second))
    x_rows = tuple((g, 0) for g in got)
    dy_rows = tuple((g, 1) for g in got)

    all_ks = (0, 1, 2)
    own0, *other0 = products(0, blk, all_ks, place, x_rows[0], dy_rows[0], weights, (packed,), 3)
    mine0, step2 = sum_over_width(own0, other0, (), (), 3)
    out0, hidden0 = grad_rows(0, blk, rows, place, gather_rows(mine0), weights)
    own1, other1 = products(1, blk, all_ks, place, x_rows[1], dy_rows[1], weights, (), 1)
    mine1, _ = sum_over_width(own1, other1, step2, (), 1)
    out1, hidden1 = grad_rows(1, blk, rows, place, gather_rows(mine1), weights)
    backs = [exchange(out0), exchange(out1)]
    grads = ()
    for e, hidden_vals in enumerate((hidden0, hidden1)):
        grads = weight_grads(e, exp_local, width, x_rows[e], dy_rows[e], hidden_vals, grads)
    grad_tokens = combine(cap, exp_local, nodes, pos, backs)
    return (grad_tokens,) + tuple(grads)


def solution(mesh):
    return jax.shard_map(
        on_device,
        mesh=mesh,
        in_specs=(
            P("node", "local"),
            P("node", "local"),
            P("node", None),
            P("node", None),
            P("node", "local", None),
            P("node", "local", None),
            P("node", None, "local"),
        ),
        out_specs=(
            P("node", "local"),
            P("node", "local", None),
            P("node", "local", None),
            P("node", None, "local"),
        ),
        check_vma=False,
    )
```

```python
import functools
import jax
import jax.numpy as jnp
from jax import lax
from jax.experimental import pallas as pl
from jax.experimental.pallas import tpu as pltpu
from jax.sharding import PartitionSpec as P

BF = jnp.bfloat16
F32 = jnp.float32
MIB = 1024 * 1024
BIG = 20
NN = (((1,), (0,)), ((), ()))
NT = (((1,), (1,)), ((), ()))
TN = (((0,), (0,)), ((), ()))


def dot(a, b, dims):
    return lax.dot_general(a, b, dims, preferred_element_type=F32)


def params(mib):
    return pltpu.CompilerParams(vmem_limit_bytes=mib * MIB)


def cost(flops, moved):
    return pl.CostEstimate(flops=flops, bytes_accessed=moved, transcendentals=0)


def whole(shape):
    return pl.BlockSpec(shape, lambda *_: (0,) * len(shape))


ANY = pl.BlockSpec(memory_space=pl.ANY)
VM = pl.BlockSpec(memory_space=pltpu.VMEM)
SM = pl.BlockSpec(memory_space=pltpu.SMEM)


def copy(src, dst, sems, i):
    c = pltpu.make_async_copy(src, dst, sems.at[i])
    c.start()
    return c


def in_vmem(x):
    return pltpu.with_memory_space_constraint(x, pltpu.VMEM)


def in_hbm(x):
    return pltpu.with_memory_space_constraint(x, pltpu.HBM)


def slot_map(ids, gates, experts):
    top, tok = ids.shape
    row = lax.broadcasted_iota(jnp.int32, (experts, tok), 0)
    named = jnp.zeros((experts, tok), F32)
    weight = jnp.zeros((experts, tok), F32)
    for k in range(top):
        hit = ids[k : k + 1, :] == row
        named = jnp.where(hit, 1.0, named)
        weight = jnp.where(hit, gates[k : k + 1, :], weight)
    at = lax.broadcasted_iota(jnp.int32, (tok, tok), 0)
    before = (at < lax.broadcasted_iota(jnp.int32, (tok, tok), 1)).astype(BF)
    pos = dot(named.astype(BF), before, NN)
    return jnp.where(named > 0.0, pos, -1.0), weight


def one_hot(pos, e, cap, exp_local, nodes):
    slot = lax.broadcasted_iota(jnp.int32, (cap, pos.shape[1]), 0).astype(F32)
    return jnp.concatenate(
        [
            (pos[n * exp_local + e : n * exp_local + e + 1, :] == slot).astype(F32)
            for n in range(nodes)
        ],
        axis=0,
    )


def pack_kernel(cap, exp_local, nodes, ids_ref, gates_ref, tok_ref, grad_ref, *refs):
    out_refs, pos_ref, out_val, sems = refs[-exp_local - 3 : -3], refs[-3], refs[-2], refs[-1]
    outs = []
    pos, weight = slot_map(ids_ref[...], gates_ref[...], exp_local * nodes)
    pos_ref[...] = pos
    width = tok_ref.shape[1]
    for e in range(exp_local):
        sel = one_hot(pos, e, cap, exp_local, nodes)
        scale = jnp.concatenate(
            [
                jnp.sum(
                    sel[n * cap : (n + 1) * cap]
                    * weight[n * exp_local + e : n * exp_local + e + 1, :],
                    axis=1,
                    keepdims=True,
                )
                for n in range(nodes)
            ],
            axis=0,
        )
        sel = sel.astype(BF)
        out_val[e, :, :width] = dot(sel, tok_ref[...], NN).astype(BF)
        out_val[e, :, width:] = (scale * dot(sel, grad_ref[...], NN)).astype(BF)
        outs.append(copy(out_val.at[e], out_refs[e], sems, e))
    for c in outs:
        c.wait()


def pack(cap, exp_local, nodes, ids, gates, tokens, out_grad, after):
    tok, width = tokens.shape
    rows = nodes * cap
    return pl.pallas_call(
        functools.partial(pack_kernel, cap, exp_local, nodes),
        out_shape=tuple(pltpu.HBM((rows, 2 * width), BF) for _ in range(exp_local))
        + (jax.ShapeDtypeStruct((exp_local * nodes, tok), F32),),
        in_specs=[VM] * 4 + [ANY] * len(after),
        out_specs=(pl.BlockSpec(memory_space=pltpu.HBM),) * exp_local + (VM,),
        scratch_shapes=[
            pltpu.VMEM((exp_local, rows, 2 * width), BF),
            pltpu.SemaphoreType.DMA((exp_local,)),
        ],
        compiler_params=params(24),
        cost_estimate=cost(1, 1),
        name="pack",
    )(in_hbm(ids.T), in_hbm(gates.T), in_hbm(tokens), in_hbm(out_grad), *after)


def slot_map(ids, gates, experts):
    top, tok = ids.shape
    row = lax.broadcasted_iota(jnp.int32, (experts, tok), 0)
    named = jnp.zeros((experts, tok), F32)
    weight = jnp.zeros((experts, tok), F32)
    for k in range(top):
        hit = ids[k : k + 1, :] == row
        named = jnp.where(hit, 1.0, named)
        weight = jnp.where(hit, gates[k : k + 1, :], weight)
    at = lax.broadcasted_iota(jnp.int32, (tok, tok), 0)
    before = (at < lax.broadcasted_iota(jnp.int32, (tok, tok), 1)).astype(BF)
    pos = dot(named.astype(BF), before, NN)
    return jnp.where(named > 0.0, pos, -1.0), weight


def one_hot(pos, e, cap, exp_local, nodes):
    slot = lax.broadcasted_iota(jnp.int32, (cap, pos.shape[1]), 0).astype(F32)
    return jnp.concatenate(
        [
            (pos[n * exp_local + e : n * exp_local + e + 1, :] == slot).astype(F32)
            for n in range(nodes)
        ],
        axis=0,
    )


def ring_slot(half, j):
    if half == 0:
        return jnp.where(j == 0, 6, jnp.where(j == 1, 4, jnp.where(j == 2, 0, 3)))
    return jnp.where(j == 0, 7, jnp.where(j == 1, 1, jnp.where(j == 2, 2, 5)))


def products_kernel(e, blk, ks, x_at, dy_at, n_after, keep, place, x_ref, dy_ref, *refs):
    w_refs = refs[:3]
    own_ref, *other_refs, x, w, wd, stage, sems, out_sems = refs[3 + n_after :]
    if keep:
        kept_ref = other_refs.pop()
    z, core = place[0], place[1]
    rows, width = x.shape[1:]
    hh = wd.shape[1]
    cols = [slice(0, hh), slice(hh, 2 * hh)]

    def rows_copy(kind):
        ref, at = ((x_ref, x_at), (dy_ref, dy_at))[kind]
        return copy(ref.at[:, at * width : (at + 1) * width], x.at[kind], sems, kind)

    def weight_copies(k):
        if k == 2:
            return [copy(w_refs[2].at[e, cols[h]], wd.at[h], sems, 6 + h) for h in range(2)]
        return [copy(w_refs[k].at[e, :, cols[h]], w.at[k, h], sems, 2 + 2 * k + h) for h in range(2)]

    x_in = {ks[0] // 2: rows_copy(ks[0] // 2)}
    w_in = {ks[0]: weight_copies(ks[0])}
    outs = []
    for k in ks:
        for h in range(2):
            if h == 0 and k in (ks[0], 2):
                x_in[k // 2].wait()
                if keep:
                    kind = slice(k // 2 * width, (k // 2 + 1) * width)
                    outs.append(copy(x.at[k // 2], kept_ref.at[:, kind], out_sems, 6 + k // 2))
            w_in[k][h].wait()
            if k == ks[0] and h == 0:
                for later in ks[1:]:
                    if later == 2:
                        x_in[1] = rows_copy(1)
                    w_in[later] = weight_copies(later)
            val = dot(x[k // 2], wd[h] if k == 2 else w[k, h], NT if k == 2 else NN).astype(BF)
            for q in range(rows // blk):
                slot = ring_slot(h, lax.rem(q // 2 - z + 4, 4))
                stage[lax.rem(q + core, 2), slot, k] = val[q * blk : (q + 1) * blk]
        outs.append(copy(
            stage.at[1, :, k],
            other_refs[0].at[:, k] if len(other_refs) == 1 else other_refs[k].at[:, 0],
            out_sems,
            2 * k + 1,
        ))
        outs.append(copy(stage.at[0, :, k], own_ref.at[:, k], out_sems, 2 * k))
    for c in outs:
        c.wait()


def products(e, blk, ks, place, x_rows, dy_rows, weights, after, pieces, keep):
    (x_arr, x_at), (dy_arr, dy_at) = x_rows, dy_rows
    at_home = in_vmem if keep else in_hbm
    rows = x_arr.shape[0]
    width, hidden = weights[0].shape[1:]
    hh = hidden // 2
    out = jax.ShapeDtypeStruct((8, 3, blk, hh), BF)
    return pl.pallas_call(
        functools.partial(products_kernel, e, blk, ks, x_at, dy_at, len(after), keep),
        out_shape=(out,)
        + tuple(jax.ShapeDtypeStruct((8, 3 // pieces, blk, hh), BF) for _ in range(pieces))
        + ((pltpu.HBM((rows, 2 * width), BF),) if keep else ()),
        in_specs=[SM] + [ANY] * (5 + len(after)),
        out_specs=[ANY] * (1 + pieces)
        + ([pl.BlockSpec(memory_space=pltpu.HBM)] if keep else []),
        scratch_shapes=[
            pltpu.VMEM((2, rows, width), BF),
            pltpu.VMEM((2, 2, width, hh), BF),
            pltpu.VMEM((2, hh, width), BF),
            pltpu.VMEM((2, 8, 3, blk, hh), BF),
            pltpu.SemaphoreType.DMA((8,)),
            pltpu.SemaphoreType.DMA((8,)),
        ],
        compiler_params=params(BIG),
        cost_estimate=cost(1, 1),
        name="products",
    )(place, at_home(x_arr), at_home(dy_arr), *[in_hbm(w) for w in weights], *after)


def swiglu_kernel(kept_ref, rm_ref, rp_ref, sp_ref, sm_ref, *refs):
    out_ref = refs[-1]
    for half, (direct, ringed) in enumerate(((rm_ref, sp_ref), (rp_ref, sm_ref))):
        gate, up, gh = [
            kept_ref[2 + half, k].astype(F32)
            + direct[1, k].astype(F32)
            + ringed[k].astype(F32)
            for k in range(3)
        ]
        sig = jax.nn.sigmoid(gate)
        act = gate * sig
        out_ref[half, 0] = (act * up).astype(BF)
        out_ref[half, 1] = (gh * up * sig * (1.0 + gate * (1.0 - sig))).astype(BF)
        out_ref[half, 2] = (gh * act).astype(BF)


def swiglu(kept, rm, rp, sp, sm, after):
    return pl.pallas_call(
        swiglu_kernel,
        out_shape=jax.ShapeDtypeStruct(rm.shape, BF),
        in_specs=[VM] * 5 + [ANY] * len(after),
        out_specs=VM,
        compiler_params=params(24),
        cost_estimate=cost(1, 1),
        name="swiglu",
    )(kept, rm, rp, sp, sm, *after)


def move(x, dz, dcore=0):
    return lax.ppermute(
        x, "local", [(i, ((i // 2 + dz) % 4) * 2 + (i + dcore) % 2) for i in range(8)]
    )


def fold_kernel(kept_ref, rp_ref, rm_ref, *refs):
    next_ref, prev_ref = refs[-2:]
    next_ref[...] = (kept_ref[0].astype(F32) + rp_ref[0].astype(F32)).astype(BF)
    prev_ref[...] = (kept_ref[1].astype(F32) + rm_ref[0].astype(F32)).astype(BF)


def fold(kept, rp, rm, after):
    out = jax.ShapeDtypeStruct(rp.shape[1:], BF)
    return pl.pallas_call(
        fold_kernel,
        out_shape=(out, out),
        in_specs=[VM] * 3 + [ANY] * len(after),
        out_specs=(VM, VM),
        compiler_params=params(24),
        cost_estimate=cost(1, 1),
        name="fold",
    )(kept, rp, rm, *after)


def add_kernel(pieces, own_ref, *refs):
    got_refs = refs[:pieces]
    outs = refs[pieces:]
    for out_ref, at in zip(outs, (0, 2, 4)):
        n = out_ref.shape[0]
        if pieces == 1:
            got = got_refs[0][at : at + n].astype(F32)
            out_ref[...] = (own_ref[at : at + n].astype(F32) + got).astype(BF)
        else:
            for k in range(3):
                got = got_refs[k][at : at + n, 0].astype(F32)
                out_ref[:, k] = (own_ref[at : at + n, k].astype(F32) + got).astype(BF)


def add(own, got):
    tail = own.shape[1:]
    return pl.pallas_call(
        functools.partial(add_kernel, len(got)),
        out_shape=tuple(jax.ShapeDtypeStruct((n,) + tail, BF) for n in (2, 2, 4)),
        compiler_params=params(24),
        cost_estimate=cost(1, 1),
        name="add",
    )(own, *got)


def sum_on_ring(own, other, swap_after, pieces):
    if pieces == 1:
        other = (tie(other, *swap_after),) if swap_after else (other,)
    got = [move(piece, 0, 1) for piece in other]
    to_next, to_prev, kept = add(own, got)
    return kept, move(to_next, 1), move(to_prev, -1)


def finish_sum(kept, rp, rm, last_after):
    add_next, add_prev = fold(kept, rp, rm, ())
    sp = move(add_next, 1)
    sm = move(add_prev, -1)
    return swiglu(kept, rm, rp, sp, sm, last_after), (sp, sm)


def tie_kernel(*refs):
    del refs


def tie(x, *others):
    return pl.pallas_call(
        tie_kernel,
        out_shape=jax.ShapeDtypeStruct(x.shape, x.dtype),
        in_specs=[ANY] * (1 + len(others)),
        out_specs=ANY,
        input_output_aliases={0: 0},
        compiler_params=params(BIG),
        cost_estimate=cost(1, 1),
        name="tie",
    )(x, *others)


def forward_rows(mine):
    prev = move(mine, 1)
    nxt = move(mine, -1)
    return mine, prev, nxt, move(prev[0], 1), move(nxt[1], -1)


def swap_rows(parts, far_after):
    late = tuple(tie(p, *far_after) for p in parts[3:]) if far_after else parts[3:]
    return parts + tuple(move(p, 0, 1) for p in parts[:3] + late)


def place_rows(blk, z, core, parts, k, dst):
    for c in range(2):
        for i, j in enumerate((0, 3, 1, 2, 2)):
            q = lax.rem(z + j, 4) * 2 + lax.rem(core + c, 2)
            at = pl.ds(pl.multiple_of(q * blk, 16), blk)
            part = parts[5 * c + i]
            for half in range(2):
                for n in range(dst.shape[0]):
                    cols = slice(half * part.shape[-1], (half + 1) * part.shape[-1])
                    if i < 3:
                        dst[n, at, cols] = part[half, k + n]
                    elif half == i - 3:
                        dst[n, at, cols] = part[k + n]


def grad_rows_kernel(e, blk, place, *refs):
    parts = refs[:10]
    wg_ref, wu_ref, out_ref, h_ref, h_val, w, out_val, sems, out_sems = refs[10:]
    w_in = [copy(w_ref.at[e], w.at[n], sems, n) for n, w_ref in enumerate((wg_ref, wu_ref))]
    place_rows(blk, place[0], place[1], parts, 0, h_val)
    w_in[0].wait()
    tot = dot(h_val[1], w[0], NT)
    w_in[1].wait()
    outs = [copy(h_val, h_ref, out_sems, 0)]
    part = out_val.shape[0] // 2
    for m in range(2):
        at = slice(m * part, (m + 1) * part)
        out_val[at] = (tot[at] + dot(h_val[2, at], w[1], NT)).astype(BF)
        outs.append(copy(out_val.at[at], out_ref.at[at], out_sems, 1 + m))
    for c in outs:
        c.wait()


def grad_rows(e, blk, rows, place, parts, weights):
    width, hidden = weights[0].shape[1:]
    return pl.pallas_call(
        functools.partial(grad_rows_kernel, e, blk),
        out_shape=(
            pltpu.HBM((rows, width), BF),
            pltpu.HBM((3, rows, hidden), BF),
        ),
        in_specs=[SM] + [VM] * 10 + [ANY] * 2,
        out_specs=(pl.BlockSpec(memory_space=pltpu.HBM),) * 2,
        scratch_shapes=[
            pltpu.VMEM((3, rows, hidden), BF),
            pltpu.VMEM((2, width, hidden), BF),
            pltpu.VMEM((rows, width), BF),
            pltpu.SemaphoreType.DMA((2,)),
            pltpu.SemaphoreType.DMA((3,)),
        ],
        compiler_params=params(BIG),
        cost_estimate=cost(1, 1),
        name="grad_rows",
    )(place, *parts, *[in_hbm(w) for w in weights[:2]])


def weight_grads_kernel(e, x_at, dy_at, x_ref, dy_ref, h_ref, *refs):
    out_refs = refs[-9:-6]
    x, h_val, dgu, dd, sems, out_sems = refs[-6:]
    width = x.shape[2]
    hh = h_val.shape[2] // 2
    cols = [slice(0, hh), slice(hh, 2 * hh)]
    x_in = [copy(x_ref.at[:, x_at * width : (x_at + 1) * width], x.at[0], sems, 0)]
    h_in = {k: copy(h_ref.at[k], h_val.at[k], sems, 2 + k) for k in (1, 2, 0)}
    x_in.append(copy(dy_ref.at[:, dy_at * width : (dy_at + 1) * width], x.at[1], sems, 1))
    outs = []
    for k in (1, 2, 0):
        h_in[k].wait()
        if k != 2:
            x_in[0 if k == 1 else 1].wait()
        for h in range(2):
            if k == 0:
                dd[h] = dot(h_val[k, :, cols[h]], x[1], TN).astype(BF)
                outs.append(copy(dd.at[h], out_refs[2].at[e, cols[h]], out_sems, 4 + h))
            else:
                dgu[k - 1, h] = dot(x[0], h_val[k, :, cols[h]], TN).astype(BF)
                outs.append(
                    copy(dgu.at[k - 1, h], out_refs[k - 1].at[e, :, cols[h]], out_sems, 2 * k - 2 + h)
                )
    for c in outs:
        c.wait()


def weight_grads(e, exp_local, width, x_rows, dy_rows, hidden_vals, into):
    (x_arr, x_at), (dy_arr, dy_at) = x_rows, dy_rows
    rows, hidden = hidden_vals.shape[1:]
    hh = hidden // 2
    up = jax.ShapeDtypeStruct((exp_local, width, hidden), BF)
    down = jax.ShapeDtypeStruct((exp_local, hidden, width), BF)
    return pl.pallas_call(
        functools.partial(weight_grads_kernel, e, x_at, dy_at),
        out_shape=(up, up, down),
        in_specs=[ANY] * (3 + len(into)),
        out_specs=[ANY] * 3,
        scratch_shapes=[
            pltpu.VMEM((2, rows, width), BF),
            pltpu.VMEM((3, rows, hidden), BF),
            pltpu.VMEM((2, 2, width, hh), BF),
            pltpu.VMEM((2, hh, width), BF),
            pltpu.SemaphoreType.DMA((5,)),
            pltpu.SemaphoreType.DMA((6,)),
        ],
        input_output_aliases={3 + i: i for i in range(len(into))},
        compiler_params=params(BIG),
        cost_estimate=cost(1, 1),
        name="weight_grads",
    )(in_hbm(x_arr), in_hbm(dy_arr), in_hbm(hidden_vals), *into)


def combine_kernel(cap, exp_local, nodes, pos_ref, *refs):
    backs, out_ref = refs[:-1], refs[-1]
    pos = pos_ref[...]
    sel = [one_hot(pos, e, cap, exp_local, nodes).astype(BF) for e in range(exp_local)]
    tot = dot(sel[0], backs[0][...], TN)
    for e in range(1, exp_local):
        tot = tot + dot(sel[e], backs[e][...], TN)
    out_ref[...] = tot.astype(BF)


def combine(cap, exp_local, nodes, pos, backs):
    tok = pos.shape[1]
    rows, width = backs[0].shape
    return pl.pallas_call(
        functools.partial(combine_kernel, cap, exp_local, nodes),
        out_shape=jax.ShapeDtypeStruct((tok, width), BF),
        compiler_params=params(24),
        cost_estimate=cost(1, 1),
        name="combine",
    )(pos, *backs)


def on_device(tokens, out_grad, expert_ids, gates, gate_weight, up_weight, down_weight):
    tok, width = tokens.shape
    top = expert_ids.shape[1]
    nodes = lax.axis_size("node")
    exp_local = gate_weight.shape[0]
    cap = tok * top * 5 // (exp_local * nodes * 4)
    rows = nodes * cap
    blk = rows // 8
    local = lax.axis_index("local")
    place = jnp.stack([local // 2, local % 2]).astype(jnp.int32)

    weights = (gate_weight, up_weight, down_weight)
    def exchange(x):
        return lax.all_to_all(x, "node", split_axis=0, concat_axis=0, tiled=True)

    pack_args = (cap, exp_local, nodes, expert_ids, gates, tokens, out_grad)
    first, second, pos = pack(*pack_args, (place,))
    got = (exchange(first), exchange(second))
    x_rows = tuple((g, 0) for g in got)
    dy_rows = tuple((g, 1) for g in got)

    all_ks = (0, 1, 2)
    own0, *other0, rows0 = products(
        0, blk, all_ks, place, x_rows[0], dy_rows[0], weights, (), 3, True
    )
    x_rows, dy_rows = ((rows0, 0), x_rows[1]), ((rows0, 1), dy_rows[1])
    mine0, step2 = finish_sum(*sum_on_ring(own0, other0, (), 3), ())
    parts0 = forward_rows(mine0)
    own1, other1 = products(1, blk, all_ks, place, x_rows[1], dy_rows[1], weights, (), 1, False)
    ring1 = sum_on_ring(own1, other1, step2, 1)
    parts0 = swap_rows(parts0, ())
    out0, hidden0 = grad_rows(0, blk, rows, place, parts0, weights)
    mine1, _ = finish_sum(*ring1, ())
    parts1 = swap_rows(forward_rows(mine1), ())
    out1, hidden1 = grad_rows(1, blk, rows, place, parts1, weights)
    backs = [exchange(out0), exchange(out1)]
    grads = ()
    for e, hidden_vals in enumerate((hidden0, hidden1)):
        grads = weight_grads(e, exp_local, width, x_rows[e], dy_rows[e], hidden_vals, grads)
    grad_tokens = combine(cap, exp_local, nodes, pos, backs)
    return (grad_tokens,) + tuple(grads)


def solution(mesh):
    return jax.shard_map(
        on_device,
        mesh=mesh,
        in_specs=(
            P("node", "local"),
            P("node", "local"),
            P("node", None),
            P("node", None),
            P("node", "local", None),
            P("node", "local", None),
            P("node", None, "local"),
        ),
        out_specs=(
            P("node", "local"),
            P("node", "local", None),
            P("node", "local", None),
            P("node", None, "local"),
        ),
        check_vma=False,
    )
```

```python
import functools
import jax
import jax.numpy as jnp
from jax import lax
from jax.experimental import pallas as pl
from jax.experimental.pallas import tpu as pltpu
from jax.sharding import PartitionSpec as P

BF = jnp.bfloat16
F32 = jnp.float32
MIB = 1024 * 1024
BIG = 20
NN = (((1,), (0,)), ((), ()))
NT = (((1,), (1,)), ((), ()))
TN = (((0,), (0,)), ((), ()))


def dot(a, b, dims):
    return lax.dot_general(a, b, dims, preferred_element_type=F32)


def params(mib):
    return pltpu.CompilerParams(vmem_limit_bytes=mib * MIB)


def cost(flops, moved):
    return pl.CostEstimate(flops=flops, bytes_accessed=moved, transcendentals=0)


def whole(shape):
    return pl.BlockSpec(shape, lambda *_: (0,) * len(shape))


ANY = pl.BlockSpec(memory_space=pl.ANY)
VM = pl.BlockSpec(memory_space=pltpu.VMEM)
SM = pl.BlockSpec(memory_space=pltpu.SMEM)


def copy(src, dst, sems, i):
    c = pltpu.make_async_copy(src, dst, sems.at[i])
    c.start()
    return c


def in_vmem(x):
    return pltpu.with_memory_space_constraint(x, pltpu.VMEM)


def in_hbm(x):
    return pltpu.with_memory_space_constraint(x, pltpu.HBM)


def slot_map(ids, gates, experts):
    top, tok = ids.shape
    row = lax.broadcasted_iota(jnp.int32, (experts, tok), 0)
    named = jnp.zeros((experts, tok), F32)
    weight = jnp.zeros((experts, tok), F32)
    for k in range(top):
        hit = ids[k : k + 1, :] == row
        named = jnp.where(hit, 1.0, named)
        weight = jnp.where(hit, gates[k : k + 1, :], weight)
    at = lax.broadcasted_iota(jnp.int32, (tok, tok), 0)
    before = (at < lax.broadcasted_iota(jnp.int32, (tok, tok), 1)).astype(BF)
    pos = dot(named.astype(BF), before, NN)
    return jnp.where(named > 0.0, pos, -1.0), weight


def one_hot(pos, e, cap, exp_local, nodes):
    slot = lax.broadcasted_iota(jnp.int32, (cap, pos.shape[1]), 0).astype(F32)
    return jnp.concatenate(
        [
            (pos[n * exp_local + e : n * exp_local + e + 1, :] == slot).astype(F32)
            for n in range(nodes)
        ],
        axis=0,
    )


def pack_kernel(cap, exp_local, nodes, ids_ref, gates_ref, tok_ref, grad_ref, *refs):
    out_refs, pos_ref, out_val, sems = refs[-exp_local - 3 : -3], refs[-3], refs[-2], refs[-1]
    outs = []
    pos, weight = slot_map(ids_ref[...], gates_ref[...], exp_local * nodes)
    pos_ref[...] = pos
    width = tok_ref.shape[1]
    for e in range(exp_local):
        sel = one_hot(pos, e, cap, exp_local, nodes)
        scale = jnp.concatenate(
            [
                jnp.sum(
                    sel[n * cap : (n + 1) * cap]
                    * weight[n * exp_local + e : n * exp_local + e + 1, :],
                    axis=1,
                    keepdims=True,
                )
                for n in range(nodes)
            ],
            axis=0,
        )
        sel = sel.astype(BF)
        for kind in range(2):
            at = slice(kind * width, (kind + 1) * width)
            picked = dot(sel, (tok_ref, grad_ref)[kind][...], NN)
            out_val[e, :, at] = (picked if kind == 0 else scale * picked).astype(BF)
            outs.append(copy(out_val.at[e, :, at], out_refs[e].at[:, at], sems, 2 * e + kind))
    for c in outs:
        c.wait()


def pack(cap, exp_local, nodes, ids, gates, tokens, out_grad, after):
    tok, width = tokens.shape
    rows = nodes * cap
    return pl.pallas_call(
        functools.partial(pack_kernel, cap, exp_local, nodes),
        out_shape=tuple(pltpu.HBM((rows, 2 * width), BF) for _ in range(exp_local))
        + (jax.ShapeDtypeStruct((exp_local * nodes, tok), F32),),
        in_specs=[VM] * 4 + [ANY] * len(after),
        out_specs=(pl.BlockSpec(memory_space=pltpu.HBM),) * exp_local + (VM,),
        scratch_shapes=[
            pltpu.VMEM((exp_local, rows, 2 * width), BF),
            pltpu.SemaphoreType.DMA((2 * exp_local,)),
        ],
        compiler_params=params(24),
        cost_estimate=cost(1, 1),
        name="pack",
    )(in_hbm(ids.T), in_hbm(gates.T), in_hbm(tokens), in_hbm(out_grad), *after)


def slot_map(ids, gates, experts):
    top, tok = ids.shape
    row = lax.broadcasted_iota(jnp.int32, (experts, tok), 0)
    named = jnp.zeros((experts, tok), F32)
    weight = jnp.zeros((experts, tok), F32)
    for k in range(top):
        hit = ids[k : k + 1, :] == row
        named = jnp.where(hit, 1.0, named)
        weight = jnp.where(hit, gates[k : k + 1, :], weight)
    at = lax.broadcasted_iota(jnp.int32, (tok, tok), 0)
    before = (at < lax.broadcasted_iota(jnp.int32, (tok, tok), 1)).astype(BF)
    pos = dot(named.astype(BF), before, NN)
    return jnp.where(named > 0.0, pos, -1.0), weight


def one_hot(pos, e, cap, exp_local, nodes):
    slot = lax.broadcasted_iota(jnp.int32, (cap, pos.shape[1]), 0).astype(F32)
    return jnp.concatenate(
        [
            (pos[n * exp_local + e : n * exp_local + e + 1, :] == slot).astype(F32)
            for n in range(nodes)
        ],
        axis=0,
    )


def ring_slot(half, j):
    if half == 0:
        return jnp.where(j == 0, 6, jnp.where(j == 1, 4, jnp.where(j == 2, 0, 3)))
    return jnp.where(j == 0, 7, jnp.where(j == 1, 1, jnp.where(j == 2, 2, 5)))


def products_kernel(e, blk, x_at, dy_at, n_after, keep, place, x_ref, dy_ref, *refs):
    w_refs = refs[:3]
    own_ref, *other_refs, x, wg, wu, wd, stage, sems, out_sems = refs[3 + n_after :]
    if keep:
        kept_ref = other_refs.pop()
    z, core = place[0], place[1]
    rows, width = x.shape[1:]
    hh = wg.shape[2]
    cols = [slice(0, hh), slice(hh, 2 * hh)]

    def rows_copy(kind):
        ref, at = ((x_ref, x_at), (dy_ref, dy_at))[kind]
        return copy(ref.at[:, at * width : (at + 1) * width], x.at[kind], sems, kind)

    def store(k, h, val):
        for q in range(rows // blk):
            slot = ring_slot(h, lax.rem(q // 2 - z + 4, 4))
            stage[lax.rem(q + core, 2), slot, k] = val[q * blk : (q + 1) * blk]

    def send(k):
        other = other_refs[0].at[:, k] if len(other_refs) == 1 else other_refs[k].at[:, 0]
        outs.append(copy(stage.at[1, :, k], other, out_sems, 2 * k + 1))
        outs.append(copy(stage.at[0, :, k], own_ref.at[:, k], out_sems, 2 * k))

    def keep_rows(kind):
        if keep:
            at = slice(kind * width, (kind + 1) * width)
            outs.append(copy(x.at[kind], kept_ref.at[:, at], out_sems, 6 + kind))

    outs = []
    x_in = rows_copy(0)
    first = copy(w_refs[0].at[e, :, cols[0]], wg.at[0], sems, 2)
    x_in.wait()
    first.wait()
    second = copy(w_refs[0].at[e, :, cols[1]], wg.at[1], sems, 3)
    up_in = copy(w_refs[1].at[e], wu, sems, 4)
    dy_in = rows_copy(1)
    down_in = copy(w_refs[2].at[e], wd, sems, 5)
    store(0, 0, dot(x[0], wg[0], NN).astype(BF))
    second.wait()
    store(0, 1, dot(x[0], wg[1], NN).astype(BF))
    send(0)
    up_in.wait()
    val = dot(x[0], wu[...], NN).astype(BF)
    for h in range(2):
        store(1, h, val[:, cols[h]])
    send(1)
    keep_rows(0)
    dy_in.wait()
    keep_rows(1)
    down_in.wait()
    val = dot(x[1], wd[...], NT).astype(BF)
    for h in range(2):
        store(2, h, val[:, cols[h]])
    send(2)
    for c in outs:
        c.wait()


def products(e, blk, place, x_rows, dy_rows, weights, after, pieces, keep):
    (x_arr, x_at), (dy_arr, dy_at) = x_rows, dy_rows
    at_home = in_vmem if keep else in_hbm
    rows = x_arr.shape[0]
    width, hidden = weights[0].shape[1:]
    hh = hidden // 2
    out = jax.ShapeDtypeStruct((8, 3, blk, hh), BF)
    return pl.pallas_call(
        functools.partial(products_kernel, e, blk, x_at, dy_at, len(after), keep),
        out_shape=(out,)
        + tuple(jax.ShapeDtypeStruct((8, 3 // pieces, blk, hh), BF) for _ in range(pieces))
        + ((pltpu.HBM((rows, 2 * width), BF),) if keep else ()),
        in_specs=[SM] + [ANY] * (5 + len(after)),
        out_specs=[ANY] * (1 + pieces)
        + ([pl.BlockSpec(memory_space=pltpu.HBM)] if keep else []),
        scratch_shapes=[
            pltpu.VMEM((2, rows, width), BF),
            pltpu.VMEM((2, width, hh), BF),
            pltpu.VMEM((width, hidden), BF),
            pltpu.VMEM((hidden, width), BF),
            pltpu.VMEM((2, 8, 3, blk, hh), BF),
            pltpu.SemaphoreType.DMA((6,)),
            pltpu.SemaphoreType.DMA((8,)),
        ],
        compiler_params=params(BIG),
        cost_estimate=cost(1, 1),
        name="products",
    )(place, at_home(x_arr), at_home(dy_arr), *[in_hbm(w) for w in weights], *after)


def swiglu_kernel(kept_ref, rm_ref, rp_ref, sp_ref, sm_ref, *refs):
    out_ref = refs[-1]
    for half, (direct, ringed) in enumerate(((rm_ref, sp_ref), (rp_ref, sm_ref))):
        gate, up, gh = [
            kept_ref[2 + half, k].astype(F32)
            + direct[1, k].astype(F32)
            + ringed[k].astype(F32)
            for k in range(3)
        ]
        sig = jax.nn.sigmoid(gate)
        act = gate * sig
        out_ref[half, 0] = (act * up).astype(BF)
        out_ref[half, 1] = (gh * up * sig * (1.0 + gate * (1.0 - sig))).astype(BF)
        out_ref[half, 2] = (gh * act).astype(BF)


def swiglu(kept, rm, rp, sp, sm, after):
    return pl.pallas_call(
        swiglu_kernel,
        out_shape=jax.ShapeDtypeStruct(rm.shape, BF),
        in_specs=[VM] * 5 + [ANY] * len(after),
        out_specs=VM,
        compiler_params=params(24),
        cost_estimate=cost(1, 1),
        name="swiglu",
    )(kept, rm, rp, sp, sm, *after)


def move(x, dz, dcore=0):
    return lax.ppermute(
        x, "local", [(i, ((i // 2 + dz) % 4) * 2 + (i + dcore) % 2) for i in range(8)]
    )


def fold_kernel(kept_ref, rp_ref, rm_ref, *refs):
    next_ref, prev_ref = refs[-2:]
    next_ref[...] = (kept_ref[0].astype(F32) + rp_ref[0].astype(F32)).astype(BF)
    prev_ref[...] = (kept_ref[1].astype(F32) + rm_ref[0].astype(F32)).astype(BF)


def fold(kept, rp, rm, after):
    out = jax.ShapeDtypeStruct(rp.shape[1:], BF)
    return pl.pallas_call(
        fold_kernel,
        out_shape=(out, out),
        in_specs=[VM] * 3 + [ANY] * len(after),
        out_specs=(VM, VM),
        compiler_params=params(24),
        cost_estimate=cost(1, 1),
        name="fold",
    )(kept, rp, rm, *after)


def add_kernel(pieces, own_ref, *refs):
    got_refs = refs[:pieces]
    outs = refs[pieces:]
    for out_ref, at in zip(outs, (0, 2, 4)):
        n = out_ref.shape[0]
        if pieces == 1:
            got = got_refs[0][at : at + n].astype(F32)
            out_ref[...] = (own_ref[at : at + n].astype(F32) + got).astype(BF)
        else:
            for k in range(3):
                got = got_refs[k][at : at + n, 0].astype(F32)
                out_ref[:, k] = (own_ref[at : at + n, k].astype(F32) + got).astype(BF)


def add(own, got):
    tail = own.shape[1:]
    return pl.pallas_call(
        functools.partial(add_kernel, len(got)),
        out_shape=tuple(jax.ShapeDtypeStruct((n,) + tail, BF) for n in (2, 2, 4)),
        compiler_params=params(24),
        cost_estimate=cost(1, 1),
        name="add",
    )(own, *got)


def sum_on_ring(own, other, swap_after, pieces):
    if pieces == 1:
        other = (tie(other, *swap_after),) if swap_after else (other,)
    got = [move(piece, 0, 1) for piece in other]
    to_next, to_prev, kept = add(own, got)
    return kept, move(to_next, 1), move(to_prev, -1)


def finish_sum(kept, rp, rm, last_after):
    add_next, add_prev = fold(kept, rp, rm, ())
    sp = move(add_next, 1)
    sm = move(add_prev, -1)
    return swiglu(kept, rm, rp, sp, sm, last_after), (sp, sm)


def tie_kernel(*refs):
    del refs


def tie(x, *others):
    return pl.pallas_call(
        tie_kernel,
        out_shape=jax.ShapeDtypeStruct(x.shape, x.dtype),
        in_specs=[ANY] * (1 + len(others)),
        out_specs=ANY,
        input_output_aliases={0: 0},
        compiler_params=params(BIG),
        cost_estimate=cost(1, 1),
        name="tie",
    )(x, *others)


def forward_rows(mine):
    prev = move(mine, 1)
    nxt = move(mine, -1)
    return mine, prev, nxt, move(prev[0], 1), move(nxt[1], -1)


def swap_rows(parts, far_after):
    late = tuple(tie(p, *far_after) for p in parts[3:]) if far_after else parts[3:]
    return parts + tuple(move(p, 0, 1) for p in parts[:3] + late)


def place_rows(blk, z, core, parts, k, dst):
    for c in range(2):
        for i, j in enumerate((0, 3, 1, 2, 2)):
            q = lax.rem(z + j, 4) * 2 + lax.rem(core + c, 2)
            at = pl.ds(pl.multiple_of(q * blk, 16), blk)
            part = parts[5 * c + i]
            for half in range(2):
                for n in range(dst.shape[0]):
                    cols = slice(half * part.shape[-1], (half + 1) * part.shape[-1])
                    if i < 3:
                        dst[n, at, cols] = part[half, k + n]
                    elif half == i - 3:
                        dst[n, at, cols] = part[k + n]


def grad_rows_kernel(e, blk, place, *refs):
    parts = refs[:10]
    wg_ref, wu_ref, out_ref, h_ref, h_val, w, out_val, sems, out_sems = refs[10:]
    w_in = [copy(w_ref.at[e], w.at[n], sems, n) for n, w_ref in enumerate((wg_ref, wu_ref))]
    place_rows(blk, place[0], place[1], parts, 0, h_val)
    w_in[0].wait()
    tot = dot(h_val[1], w[0], NT)
    w_in[1].wait()
    outs = [copy(h_val, h_ref, out_sems, 0)]
    part = out_val.shape[0] // 2
    for m in range(2):
        at = slice(m * part, (m + 1) * part)
        out_val[at] = (tot[at] + dot(h_val[2, at], w[1], NT)).astype(BF)
        outs.append(copy(out_val.at[at], out_ref.at[at], out_sems, 1 + m))
    for c in outs:
        c.wait()


def grad_rows(e, blk, rows, place, parts, weights):
    width, hidden = weights[0].shape[1:]
    return pl.pallas_call(
        functools.partial(grad_rows_kernel, e, blk),
        out_shape=(
            pltpu.HBM((rows, width), BF),
            pltpu.HBM((3, rows, hidden), BF),
        ),
        in_specs=[SM] + [VM] * 10 + [ANY] * 2,
        out_specs=(pl.BlockSpec(memory_space=pltpu.HBM),) * 2,
        scratch_shapes=[
            pltpu.VMEM((3, rows, hidden), BF),
            pltpu.VMEM((2, width, hidden), BF),
            pltpu.VMEM((rows, width), BF),
            pltpu.SemaphoreType.DMA((2,)),
            pltpu.SemaphoreType.DMA((3,)),
        ],
        compiler_params=params(BIG),
        cost_estimate=cost(1, 1),
        name="grad_rows",
    )(place, *parts, *[in_hbm(w) for w in weights[:2]])


def weight_grads_kernel(e, x_at, dy_at, x_ref, dy_ref, h_ref, *refs):
    out_refs = refs[-9:-6]
    x, h_val, dgu, dd, sems, out_sems = refs[-6:]
    width = x.shape[2]
    hh = h_val.shape[2] // 2
    cols = [slice(0, hh), slice(hh, 2 * hh)]
    x_in = [copy(x_ref.at[:, x_at * width : (x_at + 1) * width], x.at[0], sems, 0)]
    h_in = {k: copy(h_ref.at[k], h_val.at[k], sems, 2 + k) for k in (1, 2, 0)}
    x_in.append(copy(dy_ref.at[:, dy_at * width : (dy_at + 1) * width], x.at[1], sems, 1))
    outs = []
    for k in (1, 2, 0):
        h_in[k].wait()
        if k != 2:
            x_in[0 if k == 1 else 1].wait()
        for h in range(2):
            if k == 0:
                dd[h] = dot(h_val[k, :, cols[h]], x[1], TN).astype(BF)
                outs.append(copy(dd.at[h], out_refs[2].at[e, cols[h]], out_sems, 4 + h))
            else:
                dgu[k - 1, h] = dot(x[0], h_val[k, :, cols[h]], TN).astype(BF)
                outs.append(
                    copy(dgu.at[k - 1, h], out_refs[k - 1].at[e, :, cols[h]], out_sems, 2 * k - 2 + h)
                )
    for c in outs:
        c.wait()


def weight_grads(e, exp_local, width, x_rows, dy_rows, hidden_vals, into):
    (x_arr, x_at), (dy_arr, dy_at) = x_rows, dy_rows
    rows, hidden = hidden_vals.shape[1:]
    hh = hidden // 2
    up = jax.ShapeDtypeStruct((exp_local, width, hidden), BF)
    down = jax.ShapeDtypeStruct((exp_local, hidden, width), BF)
    return pl.pallas_call(
        functools.partial(weight_grads_kernel, e, x_at, dy_at),
        out_shape=(up, up, down),
        in_specs=[ANY] * (3 + len(into)),
        out_specs=[ANY] * 3,
        scratch_shapes=[
            pltpu.VMEM((2, rows, width), BF),
            pltpu.VMEM((3, rows, hidden), BF),
            pltpu.VMEM((2, 2, width, hh), BF),
            pltpu.VMEM((2, hh, width), BF),
            pltpu.SemaphoreType.DMA((5,)),
            pltpu.SemaphoreType.DMA((6,)),
        ],
        input_output_aliases={3 + i: i for i in range(len(into))},
        compiler_params=params(BIG),
        cost_estimate=cost(1, 1),
        name="weight_grads",
    )(in_hbm(x_arr), in_hbm(dy_arr), in_hbm(hidden_vals), *into)


def combine_kernel(cap, exp_local, nodes, pos_ref, *refs):
    backs, out_ref = refs[:-1], refs[-1]
    pos = pos_ref[...]
    sel = [one_hot(pos, e, cap, exp_local, nodes).astype(BF) for e in range(exp_local)]
    tot = dot(sel[0], backs[0][...], TN)
    for e in range(1, exp_local):
        tot = tot + dot(sel[e], backs[e][...], TN)
    out_ref[...] = tot.astype(BF)


def combine(cap, exp_local, nodes, pos, backs):
    tok = pos.shape[1]
    rows, width = backs[0].shape
    return pl.pallas_call(
        functools.partial(combine_kernel, cap, exp_local, nodes),
        out_shape=jax.ShapeDtypeStruct((tok, width), BF),
        compiler_params=params(24),
        cost_estimate=cost(1, 1),
        name="combine",
    )(pos, *backs)


def on_device(tokens, out_grad, expert_ids, gates, gate_weight, up_weight, down_weight):
    tok, width = tokens.shape
    top = expert_ids.shape[1]
    nodes = lax.axis_size("node")
    exp_local = gate_weight.shape[0]
    cap = tok * top * 5 // (exp_local * nodes * 4)
    rows = nodes * cap
    blk = rows // 8
    local = lax.axis_index("local")
    place = jnp.stack([local // 2, local % 2]).astype(jnp.int32)

    weights = (gate_weight, up_weight, down_weight)
    def exchange(x):
        return lax.all_to_all(x, "node", split_axis=0, concat_axis=0, tiled=True)

    pack_args = (cap, exp_local, nodes, expert_ids, gates, tokens, out_grad)
    first, second, pos = pack(*pack_args, (place,))
    got = (exchange(first), exchange(second))
    x_rows = tuple((g, 0) for g in got)
    dy_rows = tuple((g, 1) for g in got)

    own0, *other0, rows0 = products(
        0, blk, place, x_rows[0], dy_rows[0], weights, (), 3, True
    )
    x_rows, dy_rows = ((rows0, 0), x_rows[1]), ((rows0, 1), dy_rows[1])
    mine0, step2 = finish_sum(*sum_on_ring(own0, other0, (), 3), ())
    parts0 = forward_rows(mine0)
    own1, other1 = products(1, blk, place, x_rows[1], dy_rows[1], weights, (), 1, False)
    ring1 = sum_on_ring(own1, other1, step2, 1)
    parts0 = swap_rows(parts0, ())
    out0, hidden0 = grad_rows(0, blk, rows, place, parts0, weights)
    mine1, _ = finish_sum(*ring1, ())
    parts1 = swap_rows(forward_rows(mine1), ())
    out1, hidden1 = grad_rows(1, blk, rows, place, parts1, weights)
    backs = [exchange(out0), exchange(out1)]
    grads = ()
    for e, hidden_vals in enumerate((hidden0, hidden1)):
        grads = weight_grads(e, exp_local, width, x_rows[e], dy_rows[e], hidden_vals, grads)
    grad_tokens = combine(cap, exp_local, nodes, pos, backs)
    return (grad_tokens,) + tuple(grads)


def solution(mesh):
    return jax.shard_map(
        on_device,
        mesh=mesh,
        in_specs=(
            P("node", "local"),
            P("node", "local"),
            P("node", None),
            P("node", None),
            P("node", "local", None),
            P("node", "local", None),
            P("node", None, "local"),
        ),
        out_specs=(
            P("node", "local"),
            P("node", "local", None),
            P("node", "local", None),
            P("node", None, "local"),
        ),
        check_vma=False,
    )
```

```python
import functools
import jax
import jax.numpy as jnp
from jax import lax
from jax.experimental import pallas as pl
from jax.experimental.pallas import tpu as pltpu
from jax.sharding import PartitionSpec as P

BF = jnp.bfloat16
F32 = jnp.float32
MIB = 1024 * 1024
BIG = 20
NN = (((1,), (0,)), ((), ()))
NT = (((1,), (1,)), ((), ()))
TN = (((0,), (0,)), ((), ()))


def dot(a, b, dims):
    return lax.dot_general(a, b, dims, preferred_element_type=F32)


def params(mib):
    return pltpu.CompilerParams(vmem_limit_bytes=mib * MIB)


def cost(flops, moved):
    return pl.CostEstimate(flops=flops, bytes_accessed=moved, transcendentals=0)


def whole(shape):
    return pl.BlockSpec(shape, lambda *_: (0,) * len(shape))


ANY = pl.BlockSpec(memory_space=pl.ANY)
VM = pl.BlockSpec(memory_space=pltpu.VMEM)
SM = pl.BlockSpec(memory_space=pltpu.SMEM)


def copy(src, dst, sems, i):
    c = pltpu.make_async_copy(src, dst, sems.at[i])
    c.start()
    return c


def in_vmem(x):
    return pltpu.with_memory_space_constraint(x, pltpu.VMEM)


def in_hbm(x):
    return pltpu.with_memory_space_constraint(x, pltpu.HBM)


def slot_map(ids, gates, experts):
    top, tok = ids.shape
    row = lax.broadcasted_iota(jnp.int32, (experts, tok), 0)
    named = jnp.zeros((experts, tok), F32)
    weight = jnp.zeros((experts, tok), F32)
    for k in range(top):
        hit = ids[k : k + 1, :] == row
        named = jnp.where(hit, 1.0, named)
        weight = jnp.where(hit, gates[k : k + 1, :], weight)
    at = lax.broadcasted_iota(jnp.int32, (tok, tok), 0)
    before = (at < lax.broadcasted_iota(jnp.int32, (tok, tok), 1)).astype(BF)
    pos = dot(named.astype(BF), before, NN)
    return jnp.where(named > 0.0, pos, -1.0), weight


def one_hot(pos, e, cap, exp_local, nodes):
    slot = lax.broadcasted_iota(jnp.int32, (cap, pos.shape[1]), 0).astype(F32)
    return jnp.concatenate(
        [
            (pos[n * exp_local + e : n * exp_local + e + 1, :] == slot).astype(F32)
            for n in range(nodes)
        ],
        axis=0,
    )


def pack_kernel(cap, exp_local, nodes, ids_ref, gates_ref, tok_ref, grad_ref, *refs):
    out_refs, pos_ref, out_val, sems = refs[-exp_local - 3 : -3], refs[-3], refs[-2], refs[-1]
    outs = []
    pos, weight = slot_map(ids_ref[...], gates_ref[...], exp_local * nodes)
    pos_ref[...] = pos
    width = tok_ref.shape[1]
    for e in range(exp_local):
        sel = one_hot(pos, e, cap, exp_local, nodes)
        scale = jnp.concatenate(
            [
                jnp.sum(
                    sel[n * cap : (n + 1) * cap]
                    * weight[n * exp_local + e : n * exp_local + e + 1, :],
                    axis=1,
                    keepdims=True,
                )
                for n in range(nodes)
            ],
            axis=0,
        )
        sel = sel.astype(BF)
        for kind in range(2):
            at = slice(kind * width, (kind + 1) * width)
            picked = dot(sel, (tok_ref, grad_ref)[kind][...], NN)
            out_val[e, :, at] = (picked if kind == 0 else scale * picked).astype(BF)
            outs.append(copy(out_val.at[e, :, at], out_refs[e].at[:, at], sems, 2 * e + kind))
    for c in outs:
        c.wait()


def pack(cap, exp_local, nodes, ids, gates, tokens, out_grad, after):
    tok, width = tokens.shape
    rows = nodes * cap
    return pl.pallas_call(
        functools.partial(pack_kernel, cap, exp_local, nodes),
        out_shape=tuple(pltpu.HBM((rows, 2 * width), BF) for _ in range(exp_local))
        + (jax.ShapeDtypeStruct((exp_local * nodes, tok), F32),),
        in_specs=[VM] * 4 + [ANY] * len(after),
        out_specs=(pl.BlockSpec(memory_space=pltpu.HBM),) * exp_local + (VM,),
        scratch_shapes=[
            pltpu.VMEM((exp_local, rows, 2 * width), BF),
            pltpu.SemaphoreType.DMA((2 * exp_local,)),
        ],
        compiler_params=params(24),
        cost_estimate=cost(1, 1),
        name="pack",
    )(in_hbm(ids.T), in_hbm(gates.T), in_hbm(tokens), in_hbm(out_grad), *after)


def slot_map(ids, gates, experts):
    top, tok = ids.shape
    row = lax.broadcasted_iota(jnp.int32, (experts, tok), 0)
    named = jnp.zeros((experts, tok), F32)
    weight = jnp.zeros((experts, tok), F32)
    for k in range(top):
        hit = ids[k : k + 1, :] == row
        named = jnp.where(hit, 1.0, named)
        weight = jnp.where(hit, gates[k : k + 1, :], weight)
    at = lax.broadcasted_iota(jnp.int32, (tok, tok), 0)
    before = (at < lax.broadcasted_iota(jnp.int32, (tok, tok), 1)).astype(BF)
    pos = dot(named.astype(BF), before, NN)
    return jnp.where(named > 0.0, pos, -1.0), weight


def one_hot(pos, e, cap, exp_local, nodes):
    slot = lax.broadcasted_iota(jnp.int32, (cap, pos.shape[1]), 0).astype(F32)
    return jnp.concatenate(
        [
            (pos[n * exp_local + e : n * exp_local + e + 1, :] == slot).astype(F32)
            for n in range(nodes)
        ],
        axis=0,
    )


def ring_slot(half, j):
    if half == 0:
        return jnp.where(j == 0, 6, jnp.where(j == 1, 4, jnp.where(j == 2, 0, 3)))
    return jnp.where(j == 0, 7, jnp.where(j == 1, 1, jnp.where(j == 2, 2, 5)))


def products_kernel(e, blk, x_at, dy_at, n_after, keep, place, x_ref, dy_ref, *refs):
    w_refs = refs[:3]
    own_ref, *other_refs, x, wg, wu, wd, stage, sems, out_sems = refs[3 + n_after :]
    if keep:
        kept_ref = other_refs.pop()
    z, core = place[0], place[1]
    rows, width = x.shape[1:]
    hh = wg.shape[2]
    cols = [slice(0, hh), slice(hh, 2 * hh)]

    def rows_copy(kind):
        ref, at = ((x_ref, x_at), (dy_ref, dy_at))[kind]
        return copy(ref.at[:, at * width : (at + 1) * width], x.at[kind], sems, kind)

    def store(k, h, val):
        for q in range(rows // blk):
            slot = ring_slot(h, lax.rem(q // 2 - z + 4, 4))
            stage[lax.rem(q + core, 2), slot, k] = val[q * blk : (q + 1) * blk]

    def send(k):
        other = other_refs[0].at[:, k] if len(other_refs) == 1 else other_refs[k].at[:, 0]
        outs.append(copy(stage.at[1, :, k], other, out_sems, 2 * k + 1))
        outs.append(copy(stage.at[0, :, k], own_ref.at[:, k], out_sems, 2 * k))

    def keep_rows(kind):
        if keep:
            at = slice(kind * width, (kind + 1) * width)
            outs.append(copy(x.at[kind], kept_ref.at[:, at], out_sems, 6 + kind))

    outs = []
    x_in = rows_copy(0)
    first = copy(w_refs[0].at[e, :, cols[0]], wg.at[0], sems, 2)
    x_in.wait()
    first.wait()
    second = copy(w_refs[0].at[e, :, cols[1]], wg.at[1], sems, 3)
    up_in = copy(w_refs[1].at[e], wu, sems, 4)
    dy_in = rows_copy(1)
    down_in = copy(w_refs[2].at[e], wd, sems, 5)
    store(0, 0, dot(x[0], wg[0], NN).astype(BF))
    second.wait()
    store(0, 1, dot(x[0], wg[1], NN).astype(BF))
    send(0)
    up_in.wait()
    val = dot(x[0], wu[...], NN).astype(BF)
    for h in range(2):
        store(1, h, val[:, cols[h]])
    send(1)
    keep_rows(0)
    dy_in.wait()
    keep_rows(1)
    down_in.wait()
    val = dot(x[1], wd[...], NT).astype(BF)
    for h in range(2):
        store(2, h, val[:, cols[h]])
    send(2)
    for c in outs:
        c.wait()


def products(e, blk, place, x_rows, dy_rows, weights, after, pieces, keep):
    (x_arr, x_at), (dy_arr, dy_at) = x_rows, dy_rows
    at_home = in_vmem if keep else in_hbm
    rows = x_arr.shape[0]
    width, hidden = weights[0].shape[1:]
    hh = hidden // 2
    out = jax.ShapeDtypeStruct((8, 3, blk, hh), BF)
    return pl.pallas_call(
        functools.partial(products_kernel, e, blk, x_at, dy_at, len(after), keep),
        out_shape=(out,)
        + tuple(jax.ShapeDtypeStruct((8, 3 // pieces, blk, hh), BF) for _ in range(pieces))
        + ((pltpu.HBM((rows, 2 * width), BF),) if keep else ()),
        in_specs=[SM] + [ANY] * (5 + len(after)),
        out_specs=[ANY] * (1 + pieces)
        + ([pl.BlockSpec(memory_space=pltpu.HBM)] if keep else []),
        scratch_shapes=[
            pltpu.VMEM((2, rows, width), BF),
            pltpu.VMEM((2, width, hh), BF),
            pltpu.VMEM((width, hidden), BF),
            pltpu.VMEM((hidden, width), BF),
            pltpu.VMEM((2, 8, 3, blk, hh), BF),
            pltpu.SemaphoreType.DMA((6,)),
            pltpu.SemaphoreType.DMA((8,)),
        ],
        compiler_params=params(BIG),
        cost_estimate=cost(1, 1),
        name="products",
    )(place, at_home(x_arr), at_home(dy_arr), *[in_hbm(w) for w in weights], *after)


def write_hidden(out_ref, half, totals):
    gate, up, gh = totals
    sig = jax.nn.sigmoid(gate)
    act = gate * sig
    out_ref[half, 0] = (act * up).astype(BF)
    out_ref[half, 1] = (gh * up * sig * (1.0 + gate * (1.0 - sig))).astype(BF)
    out_ref[half, 2] = (gh * act).astype(BF)


def swiglu_kernel(kept_ref, rm_ref, rp_ref, sp_ref, sm_ref, *refs):
    for half, (direct, ringed) in enumerate(((rm_ref, sp_ref), (rp_ref, sm_ref))):
        totals = [
            kept_ref[2 + half, k].astype(F32)
            + direct[1, k].astype(F32)
            + ringed[k].astype(F32)
            for k in range(3)
        ]
        write_hidden(refs[-1], half, totals)


def swiglu_direct_kernel(own_ref, *refs):
    for half in range(2):
        totals = [own_ref[half, k].astype(F32) for k in range(3)]
        for ref in refs[:-1]:
            totals = [t + ref[half, k].astype(F32) for k, t in enumerate(totals)]
        write_hidden(refs[-1], half, totals)


def sum_directly(own, other):
    got = [move(piece, 0, 1) for piece in other]
    *sent, mine = add(DIRECT, own, got)
    came = tuple(move(x, dz) for x, dz in zip(sent, (1, -1, 2)))
    out = pl.pallas_call(
        swiglu_direct_kernel,
        out_shape=jax.ShapeDtypeStruct(mine.shape, BF),
        in_specs=[VM] * 4,
        out_specs=VM,
        compiler_params=params(24),
        cost_estimate=cost(1, 1),
        name="swiglu",
    )(mine, *came)
    return out, came


def swiglu(kept, rm, rp, sp, sm, after):
    return pl.pallas_call(
        swiglu_kernel,
        out_shape=jax.ShapeDtypeStruct(rm.shape, BF),
        in_specs=[VM] * 5 + [ANY] * len(after),
        out_specs=VM,
        compiler_params=params(24),
        cost_estimate=cost(1, 1),
        name="swiglu",
    )(kept, rm, rp, sp, sm, *after)


def move(x, dz, dcore=0):
    return lax.ppermute(
        x, "local", [(i, ((i // 2 + dz) % 4) * 2 + (i + dcore) % 2) for i in range(8)]
    )


def fold_kernel(kept_ref, rp_ref, rm_ref, *refs):
    next_ref, prev_ref = refs[-2:]
    next_ref[...] = (kept_ref[0].astype(F32) + rp_ref[0].astype(F32)).astype(BF)
    prev_ref[...] = (kept_ref[1].astype(F32) + rm_ref[0].astype(F32)).astype(BF)


def fold(kept, rp, rm, after):
    out = jax.ShapeDtypeStruct(rp.shape[1:], BF)
    return pl.pallas_call(
        fold_kernel,
        out_shape=(out, out),
        in_specs=[VM] * 3 + [ANY] * len(after),
        out_specs=(VM, VM),
        compiler_params=params(24),
        cost_estimate=cost(1, 1),
        name="fold",
    )(kept, rp, rm, *after)


RING = ((0, 1), (2, 3), (4, 5, 6, 7))
DIRECT = ((4, 1), (3, 5), (0, 2), (6, 7))


def add_kernel(groups, pieces, own_ref, *refs):
    got_refs = refs[:pieces]
    for out_ref, slots in zip(refs[pieces:], groups):
        for i, slot in enumerate(slots):
            for k in range(3):
                got = got_refs[0][slot, k] if pieces == 1 else got_refs[k][slot, 0]
                out_ref[i, k] = (own_ref[slot, k].astype(F32) + got.astype(F32)).astype(BF)


def add(groups, own, got):
    tail = own.shape[1:]
    return pl.pallas_call(
        functools.partial(add_kernel, groups, len(got)),
        out_shape=tuple(jax.ShapeDtypeStruct((len(g),) + tail, BF) for g in groups),
        compiler_params=params(24),
        cost_estimate=cost(1, 1),
        name="add",
    )(own, *got)


def sum_on_ring(own, other, swap_after, pieces):
    if pieces == 1:
        other = (tie(other, *swap_after),) if swap_after else (other,)
    got = [move(piece, 0, 1) for piece in other]
    to_next, to_prev, kept = add(RING, own, got)
    return kept, move(to_next, 1), move(to_prev, -1)


def finish_sum(kept, rp, rm, last_after):
    add_next, add_prev = fold(kept, rp, rm, ())
    sp = move(add_next, 1)
    sm = move(add_prev, -1)
    return swiglu(kept, rm, rp, sp, sm, last_after), (sp, sm)


def tie_kernel(*refs):
    del refs


def tie(x, *others):
    return pl.pallas_call(
        tie_kernel,
        out_shape=jax.ShapeDtypeStruct(x.shape, x.dtype),
        in_specs=[ANY] * (1 + len(others)),
        out_specs=ANY,
        input_output_aliases={0: 0},
        compiler_params=params(BIG),
        cost_estimate=cost(1, 1),
        name="tie",
    )(x, *others)


def forward_rows(mine):
    prev = move(mine, 1)
    nxt = move(mine, -1)
    return mine, prev, nxt, move(prev[0], 1), move(nxt[1], -1)


def swap_rows(parts, far_after):
    late = tuple(tie(p, *far_after) for p in parts[3:]) if far_after else parts[3:]
    return parts + tuple(move(p, 0, 1) for p in parts[:3] + late)


def place_rows(blk, z, core, parts, k, dst):
    for c in range(2):
        for i, j in enumerate((0, 3, 1, 2, 2)):
            q = lax.rem(z + j, 4) * 2 + lax.rem(core + c, 2)
            at = pl.ds(pl.multiple_of(q * blk, 16), blk)
            part = parts[5 * c + i]
            for half in range(2):
                for n in range(dst.shape[0]):
                    cols = slice(half * part.shape[-1], (half + 1) * part.shape[-1])
                    if i < 3:
                        dst[n, at, cols] = part[half, k + n]
                    elif half == i - 3:
                        dst[n, at, cols] = part[k + n]


def grad_rows_kernel(e, blk, place, *refs):
    parts = refs[:10]
    wg_ref, wu_ref, out_ref, h_ref, h_val, w, out_val, sems, out_sems = refs[10:]
    w_in = [copy(w_ref.at[e], w.at[n], sems, n) for n, w_ref in enumerate((wg_ref, wu_ref))]
    place_rows(blk, place[0], place[1], parts, 0, h_val)
    w_in[0].wait()
    tot = dot(h_val[1], w[0], NT)
    w_in[1].wait()
    outs = [copy(h_val, h_ref, out_sems, 0)]
    part = out_val.shape[0] // 2
    for m in range(2):
        at = slice(m * part, (m + 1) * part)
        out_val[at] = (tot[at] + dot(h_val[2, at], w[1], NT)).astype(BF)
        outs.append(copy(out_val.at[at], out_ref.at[at], out_sems, 1 + m))
    for c in outs:
        c.wait()


def grad_rows(e, blk, rows, place, parts, weights):
    width, hidden = weights[0].shape[1:]
    return pl.pallas_call(
        functools.partial(grad_rows_kernel, e, blk),
        out_shape=(
            pltpu.HBM((rows, width), BF),
            pltpu.HBM((3, rows, hidden), BF),
        ),
        in_specs=[SM] + [VM] * 10 + [ANY] * 2,
        out_specs=(pl.BlockSpec(memory_space=pltpu.HBM),) * 2,
        scratch_shapes=[
            pltpu.VMEM((3, rows, hidden), BF),
            pltpu.VMEM((2, width, hidden), BF),
            pltpu.VMEM((rows, width), BF),
            pltpu.SemaphoreType.DMA((2,)),
            pltpu.SemaphoreType.DMA((3,)),
        ],
        compiler_params=params(BIG),
        cost_estimate=cost(1, 1),
        name="grad_rows",
    )(place, *parts, *[in_hbm(w) for w in weights[:2]])


def weight_grads_kernel(e, x_at, dy_at, x_ref, dy_ref, h_ref, *refs):
    out_refs = refs[-9:-6]
    x, h_val, dgu, dd, sems, out_sems = refs[-6:]
    width = x.shape[2]
    hh = h_val.shape[2] // 2
    cols = [slice(0, hh), slice(hh, 2 * hh)]
    x_in = [copy(x_ref.at[:, x_at * width : (x_at + 1) * width], x.at[0], sems, 0)]
    h_in = {k: copy(h_ref.at[k], h_val.at[k], sems, 2 + k) for k in (1, 2, 0)}
    x_in.append(copy(dy_ref.at[:, dy_at * width : (dy_at + 1) * width], x.at[1], sems, 1))
    outs = []
    for k in (1, 2, 0):
        h_in[k].wait()
        if k != 2:
            x_in[0 if k == 1 else 1].wait()
        for h in range(2):
            if k == 0:
                dd[h] = dot(h_val[k, :, cols[h]], x[1], TN).astype(BF)
                outs.append(copy(dd.at[h], out_refs[2].at[e, cols[h]], out_sems, 4 + h))
            else:
                dgu[k - 1, h] = dot(x[0], h_val[k, :, cols[h]], TN).astype(BF)
                outs.append(
                    copy(dgu.at[k - 1, h], out_refs[k - 1].at[e, :, cols[h]], out_sems, 2 * k - 2 + h)
                )
    for c in outs:
        c.wait()


def weight_grads(e, exp_local, width, x_rows, dy_rows, hidden_vals, into):
    (x_arr, x_at), (dy_arr, dy_at) = x_rows, dy_rows
    rows, hidden = hidden_vals.shape[1:]
    hh = hidden // 2
    up = jax.ShapeDtypeStruct((exp_local, width, hidden), BF)
    down = jax.ShapeDtypeStruct((exp_local, hidden, width), BF)
    return pl.pallas_call(
        functools.partial(weight_grads_kernel, e, x_at, dy_at),
        out_shape=(up, up, down),
        in_specs=[ANY] * (3 + len(into)),
        out_specs=[ANY] * 3,
        scratch_shapes=[
            pltpu.VMEM((2, rows, width), BF),
            pltpu.VMEM((3, rows, hidden), BF),
            pltpu.VMEM((2, 2, width, hh), BF),
            pltpu.VMEM((2, hh, width), BF),
            pltpu.SemaphoreType.DMA((5,)),
            pltpu.SemaphoreType.DMA((6,)),
        ],
        input_output_aliases={3 + i: i for i in range(len(into))},
        compiler_params=params(BIG),
        cost_estimate=cost(1, 1),
        name="weight_grads",
    )(in_hbm(x_arr), in_hbm(dy_arr), in_hbm(hidden_vals), *into)


def combine_kernel(cap, exp_local, nodes, pos_ref, *refs):
    backs, out_ref = refs[:-1], refs[-1]
    pos = pos_ref[...]
    sel = [one_hot(pos, e, cap, exp_local, nodes).astype(BF) for e in range(exp_local)]
    tot = dot(sel[0], backs[0][...], TN)
    for e in range(1, exp_local):
        tot = tot + dot(sel[e], backs[e][...], TN)
    out_ref[...] = tot.astype(BF)


def combine(cap, exp_local, nodes, pos, backs):
    tok = pos.shape[1]
    rows, width = backs[0].shape
    return pl.pallas_call(
        functools.partial(combine_kernel, cap, exp_local, nodes),
        out_shape=jax.ShapeDtypeStruct((tok, width), BF),
        compiler_params=params(24),
        cost_estimate=cost(1, 1),
        name="combine",
    )(pos, *backs)


def on_device(tokens, out_grad, expert_ids, gates, gate_weight, up_weight, down_weight):
    tok, width = tokens.shape
    top = expert_ids.shape[1]
    nodes = lax.axis_size("node")
    exp_local = gate_weight.shape[0]
    cap = tok * top * 5 // (exp_local * nodes * 4)
    rows = nodes * cap
    blk = rows // 8
    local = lax.axis_index("local")
    place = jnp.stack([local // 2, local % 2]).astype(jnp.int32)

    weights = (gate_weight, up_weight, down_weight)
    def exchange(x):
        return lax.all_to_all(x, "node", split_axis=0, concat_axis=0, tiled=True)

    pack_args = (cap, exp_local, nodes, expert_ids, gates, tokens, out_grad)
    first, second, pos = pack(*pack_args, (place,))
    got = (exchange(first), exchange(second))
    x_rows = tuple((g, 0) for g in got)
    dy_rows = tuple((g, 1) for g in got)

    own0, *other0, rows0 = products(
        0, blk, place, x_rows[0], dy_rows[0], weights, (), 3, True
    )
    x_rows, dy_rows = ((rows0, 0), x_rows[1]), ((rows0, 1), dy_rows[1])
    mine0, step2 = sum_directly(own0, other0)
    parts0 = forward_rows(mine0)
    own1, other1 = products(1, blk, place, x_rows[1], dy_rows[1], weights, (), 1, False)
    ring1 = sum_on_ring(own1, other1, step2, 1)
    parts0 = swap_rows(parts0, ())
    out0, hidden0 = grad_rows(0, blk, rows, place, parts0, weights)
    mine1, _ = finish_sum(*ring1, ())
    parts1 = swap_rows(forward_rows(mine1), ())
    out1, hidden1 = grad_rows(1, blk, rows, place, parts1, weights)
    backs = [exchange(out0), exchange(out1)]
    grads = ()
    for e, hidden_vals in enumerate((hidden0, hidden1)):
        grads = weight_grads(e, exp_local, width, x_rows[e], dy_rows[e], hidden_vals, grads)
    grad_tokens = combine(cap, exp_local, nodes, pos, backs)
    return (grad_tokens,) + tuple(grads)


def solution(mesh):
    return jax.shard_map(
        on_device,
        mesh=mesh,
        in_specs=(
            P("node", "local"),
            P("node", "local"),
            P("node", None),
            P("node", None),
            P("node", "local", None),
            P("node", "local", None),
            P("node", None, "local"),
        ),
        out_specs=(
            P("node", "local"),
            P("node", "local", None),
            P("node", "local", None),
            P("node", None, "local"),
        ),
        check_vma=False,
    )
```
